32 devices in a mesh: dp: 8 (over y, x, core), tp: 4 (over z).
Axes of the slice: x: 2, y: 2, z: 4, core: 2. Of those that a mesh axis runs over, the one named last changes fastest.
Arguments:
- residual_hidden: bfloat16 [64, 4096], P('dp'), may hold values from -6 to 6
- attention_norm_gain: float32 [4096], replicated, may hold values from 0.25 to 1.75
- query_matrix: bfloat16 [4096, 8192], P(None, 'tp'), may hold values from -0.09375 to 0.09375
- key_matrix: bfloat16 [4096, 1024], P(None, 'tp'), may hold values from -0.09375 to 0.09375
- value_matrix: bfloat16 [4096, 1024], P(None, 'tp'), may hold values from -0.09375 to 0.09375
- output_matrix: bfloat16 [8192, 4096], P('tp'), may hold values from -0.5 to 0.5
- query_adapter_down: bfloat16 [4096, 64], P(('dp', 'tp')), may hold values from -0.09375 to 0.09375
- query_adapter_up: bfloat16 [64, 8192], P(None, ('tp', 'dp')), may hold values from -0.375 to 0.375
- output_adapter_down: bfloat16 [8192, 64], P(('tp', 'dp')), may hold values from -0.5 to 0.5
- output_adapter_up: bfloat16 [64, 4096], P(None, ('tp', 'dp')), may hold values from -0.375 to 0.375
- cached_rotated_keys: bfloat16 [64, 8, 1024, 128], P('dp', 'tp'), as said below
- cached_value_rows: bfloat16 [64, 8, 1024, 128], P('dp', 'tp'), may hold values from -6 to 6
- cache_fill_lengths: int32 [64], P('dp'), may hold values from 1 to 1024, 32768 in all
Outputs:
- attn_out: float32 [64, 4096], P('dp', 'tp')
The draws below stay inside these ranges and needn't reach their ends.
Inputs may be any that keep to these rules, and one draw needn't show every extreme that they name: Cache positions at or above a row's length hold no key of that row; the new token stands at position cache_fill_lengths. `cached_rotated_keys`: keys are already rotated to their positions.
All inputs are finite; a program needn't handle non-finite values. No bound on the sum of `cache_fill_lengths` on one device may be relied on, other than what follows from the above.
Results may differ from the reference program's by a relative error of at most 0.004.
The reference program's roundings to bfloat16 on the way count: a program that leaves them out, or rounds other values in their place, can miss the bound.
Values may be sent and summed in bfloat16 or wider, within the bound.
A program may use at most 128 MiB of HBM per device.

```python
import math
import jax
import jax.numpy as jnp
import numpy as np
from jax import lax

MODEL_FEATURES = 4096
HQ = 64
KVH = 8
HEAD_SIZE = 128
ADAPTER_RANK = 64
CACHE = 1024
ROWS = 64
QUERY_FEATURES = 8192
KW = 1024


def draw_cached_rotated_keys(key, part):
    key = jax.random.fold_in(key, 7)
    base = jax.random.truncated_normal(key, -6.0, 6.0, (ROWS, KVH, CACHE, HEAD_SIZE), jnp.float32)
    return base.astype(jnp.bfloat16)


def block_levels(rng, shape, cuts, smallest, largest):
    def one(axis_at, shards_of):
        heights = jax.random.uniform(jax.random.fold_in(jax.random.fold_in(rng, 6), axis_at), (shards_of,), jnp.float32, smallest / len(cuts), largest / len(cuts))
        return jnp.repeat(jnp.exp(heights), shape[axis_at] // shards_of).reshape((-1,) + (1,) * (len(shape) - axis_at - 1))

    gain = one(*cuts[0])
    for cut in cuts[1:]:
        gain = gain * one(*cut)
    return gain


def length_profile(amount, total, reach, lean):
    loads = [(1 << 20) // math.isqrt(grade ** lean) + 1 for grade in range(2, amount + 1)]
    surplus, given = total - reach - (amount - 1), [1] * (amount - 1)
    while surplus > 0:
        free = [i for i in range(amount - 1) if given[i] < reach]
        whole, budget = sum([loads[i] for i in free]), surplus
        for i in free:
            extra = min(reach - given[i], max(1, budget * loads[i] // whole), surplus)
            given[i] = given[i] + extra
            surplus = surplus - extra
    return np.array([reach] + given)


def ragged(stream_key, count, total, most, skew):
    if count == 2:
        one = jax.random.randint(stream_key, (), max(1, total - most), min(most, total - 1) + 1)
        return jnp.stack([one, total - one])
    lengths = jnp.asarray(length_profile(count, total, most, skew), jnp.int32)
    couples = (count - 1) // 2
    donor, taker = lengths[1:1 + 2 * couples:2], lengths[2:2 + 2 * couples:2]
    slack = jnp.minimum(donor - 1, most - taker)
    passed = jax.random.randint(jax.random.fold_in(stream_key, 1), (couples,), 0, 1 << 20) % (slack + 1)
    lengths = lengths.at[1:1 + 2 * couples:2].set(donor - passed).at[2:2 + 2 * couples:2].set(taker + passed)
    return lengths[jax.random.permutation(jax.random.fold_in(stream_key, 2), count)]


def bell_draw(key, extent, deviation, reach, split=(), held_as=jnp.bfloat16):
    gain = block_levels(key, extent, split, -0.22, 0.18) if split else 1.0
    values = jax.random.normal(key, extent, jnp.float32) * deviation * gain
    return jnp.minimum(jnp.maximum(values, -reach), reach).astype(held_as)


def setup_inputs(seed: int = 0) -> dict:
    seeds = jax.random.split(jax.random.key(seed), 14)
    return {
        "residual_hidden": bell_draw(seeds[0], (ROWS, MODEL_FEATURES), 1.0, 6.0, ((0, 8),)),
        "attention_norm_gain": jnp.clip(1.0 + 0.15 * jax.random.normal(seeds[1], (MODEL_FEATURES,), jnp.float32), 0.25, 1.75),
        "query_matrix": bell_draw(seeds[2], (MODEL_FEATURES, QUERY_FEATURES), MODEL_FEATURES ** -0.5, 0.09375, ((1, 4),)),
        "key_matrix": bell_draw(seeds[3], (MODEL_FEATURES, KW), MODEL_FEATURES ** -0.5, 0.09375, ((1, 4),)),
        "value_matrix": bell_draw(seeds[4], (MODEL_FEATURES, KW), MODEL_FEATURES ** -0.5, 0.09375, ((1, 4),)),
        "output_matrix": bell_draw(seeds[5], (QUERY_FEATURES, MODEL_FEATURES), HEAD_SIZE ** -0.5, 0.5, ((0, 4),)),
        "query_adapter_down": bell_draw(seeds[6], (MODEL_FEATURES, ADAPTER_RANK), MODEL_FEATURES ** -0.5, 0.09375, ((0, 32),)),
        "query_adapter_up": bell_draw(seeds[7], (ADAPTER_RANK, QUERY_FEATURES), (4 * ADAPTER_RANK) ** -0.5, 0.375, ((1, 32),)),
        "output_adapter_down": bell_draw(seeds[8], (QUERY_FEATURES, ADAPTER_RANK), HEAD_SIZE ** -0.5, 0.5, ((0, 32),)),
        "output_adapter_up": bell_draw(seeds[9], (ADAPTER_RANK, MODEL_FEATURES), (4 * ADAPTER_RANK) ** -0.5, 0.375, ((1, 32),)),
        "cached_rotated_keys": draw_cached_rotated_keys(jax.random.fold_in(seeds[13], 71), 0),
        "cached_value_rows": bell_draw(seeds[11], (ROWS, KVH, CACHE, HEAD_SIZE), 1.0, 6.0, ((0, 8), (1, 4))),
        "cache_fill_lengths": ragged(seeds[12], ROWS, ROWS * CACHE // 2, CACHE, 0).astype(jnp.int32),
    }


adapter_scale = 2.0
rope_theta = 500000.0

def rotate(vectors, positions):
    half_dim = vectors.shape[-1] // 2
    steps_idx = jnp.arange(half_dim, dtype=jnp.float32)
    inverse = jnp.exp(steps_idx * (-2.0 * math.log(rope_theta) / vectors.shape[-1]))
    angles = positions[:, None, None] * inverse[None, None, :]
    cosine = jnp.cos(angles)
    sine = jnp.sin(angles)
    first = vectors[..., :half_dim]
    second = vectors[..., half_dim:]
    return jnp.concatenate([first * cosine - second * sine, second * cosine + first * sine], axis=-1)

def reference(residual_hidden, attention_norm_gain, query_matrix, key_matrix, value_matrix, output_matrix, query_adapter_down, query_adapter_up, output_adapter_down, output_adapter_up, cached_rotated_keys, cached_value_rows, cache_fill_lengths):
    hidden_f = residual_hidden.astype(jnp.float32)
    normalized_hidden = (hidden_f * lax.rsqrt(lax.optimization_barrier(jnp.mean(hidden_f * hidden_f, axis=-1, keepdims=True)) + 1e-05) * attention_norm_gain).astype(jnp.bfloat16)
    query_low_rank = jnp.dot(normalized_hidden, query_adapter_down, preferred_element_type=jnp.float32)
    query_rows = jnp.dot(normalized_hidden, query_matrix, preferred_element_type=jnp.float32) + adapter_scale * jnp.dot(query_low_rank, query_adapter_up.astype(jnp.float32), precision=lax.Precision.HIGHEST)
    keys_new = jnp.dot(normalized_hidden, key_matrix, preferred_element_type=jnp.float32)
    values_new = jnp.dot(normalized_hidden, value_matrix, preferred_element_type=jnp.float32).astype(jnp.bfloat16)
    positions = cache_fill_lengths.astype(jnp.float32)
    group_size = HQ // KVH
    query_rot = rotate(query_rows.reshape(ROWS, HQ, HEAD_SIZE), positions).astype(jnp.bfloat16).reshape(ROWS, KVH, group_size, HEAD_SIZE)
    key_rot = rotate(keys_new.reshape(ROWS, KVH, HEAD_SIZE), positions).astype(jnp.bfloat16)
    value_rows = values_new.reshape(ROWS, KVH, HEAD_SIZE)
    score_scale = HEAD_SIZE ** (-0.5)
    query_f = query_rot.astype(jnp.float32)
    scores = jnp.einsum('rkgd,rkcd->rkgc', query_f, cached_rotated_keys.astype(jnp.float32)) * score_scale
    visible = jnp.arange(CACHE, dtype=jnp.int32)[None, None, None, :] < cache_fill_lengths.astype(jnp.int32)[:, None, None, None]
    scores = jnp.where(visible, scores, -jnp.inf)
    own_score = jnp.einsum('rkgd,rkd->rkg', query_f, key_rot.astype(jnp.float32)) * score_scale
    top_score = jnp.maximum(lax.optimization_barrier(jnp.max(scores, axis=-1)), own_score)
    cache_exp = jnp.exp(scores - top_score[..., None])
    own_exp = jnp.exp(own_score - top_score)
    denominator = lax.optimization_barrier(jnp.sum(cache_exp, axis=-1)) + own_exp
    cache_weight = (cache_exp / denominator[..., None]).astype(jnp.bfloat16)
    own_weight = (own_exp / denominator).astype(jnp.bfloat16)
    attn = jnp.einsum('rkgc,rkcd->rkgd', cache_weight.astype(jnp.float32), cached_value_rows.astype(jnp.float32))
    attn = attn + own_weight.astype(jnp.float32)[..., None] * value_rows.astype(jnp.float32)[:, :, None, :]
    attention_flattened = attn.astype(jnp.bfloat16).reshape(ROWS, QUERY_FEATURES)
    output_low_rank = jnp.dot(attention_flattened, output_adapter_down, preferred_element_type=jnp.float32)
    return jnp.dot(attention_flattened, output_matrix, preferred_element_type=jnp.float32) + adapter_scale * jnp.dot(output_low_rank, output_adapter_up.astype(jnp.float32), precision=lax.Precision.HIGHEST)
```

```python
import functools
import math

import jax
import jax.numpy as jnp
from jax import lax
from jax.experimental import pallas as pl
from jax.experimental.pallas import tpu as pltpu
from jax.sharding import PartitionSpec as P

HEAD_SIZE = 128


adapter_scale = 2.0
rope_theta = 500000.0


def rotate(vectors, positions):
    half_dim = vectors.shape[-1] // 2
    steps_idx = jnp.arange(half_dim, dtype=jnp.float32)
    inverse = jnp.exp(steps_idx * (-2.0 * math.log(rope_theta) / vectors.shape[-1]))
    angles = positions[:, None, None] * inverse[None, None, :]
    cosine = jnp.cos(angles)
    sine = jnp.sin(angles)
    first = vectors[..., :half_dim]
    second = vectors[..., half_dim:]
    return jnp.concatenate(
        [first * cosine - second * sine, second * cosine + first * sine], axis=-1
    )


def on_device_narrow(
    residual_hidden,
    attention_norm_gain,
    query_matrix,
    key_matrix,
    value_matrix,
    output_matrix,
    query_adapter_down,
    query_adapter_up,
    output_adapter_down,
    output_adapter_up,
    cached_rotated_keys,
    cached_value_rows,
    cache_fill_lengths,
):
    row_count = residual_hidden.shape[0]
    feature_width = residual_hidden.shape[1]
    rank_width = query_adapter_down.shape[1]
    local_heads = query_matrix.shape[1] // HEAD_SIZE
    local_groups = key_matrix.shape[1] // HEAD_SIZE
    group_size = local_heads // local_groups
    cache_length = cached_rotated_keys.shape[2]
    hidden_f = residual_hidden.astype(jnp.float32)
    normalized_hidden = (
        hidden_f
        * lax.rsqrt(jnp.mean(hidden_f * hidden_f, axis=-1, keepdims=True) + 1e-05)
        * attention_norm_gain
    ).astype(jnp.bfloat16)
    q_up_local, o_down_local = (
        lax.all_gather(query_adapter_up, "dp", axis=1, tiled=True),
        lax.all_gather(output_adapter_down, "dp", axis=0, tiled=True),
    )
    q_down_share = lax.all_gather(query_adapter_down, "dp", axis=0, tiled=True)
    dp_count = lax.axis_size("dp")
    tp_count = lax.axis_size("tp")
    block_width = feature_width // (dp_count * tp_count)
    picked = lax.dynamic_index_in_dim(
        normalized_hidden.reshape(row_count, dp_count, tp_count, block_width),
        lax.axis_index("tp"),
        2,
        keepdims=False,
    )
    partial_low = jnp.einsum(
        "rdb,dbk->rk",
        picked,
        q_down_share.reshape(dp_count, block_width, rank_width),
        preferred_element_type=jnp.float32,
    )
    query_low_rank = lax.psum(partial_low, "tp")
    query_rows = jnp.dot(
        normalized_hidden, query_matrix, preferred_element_type=jnp.float32
    ) + adapter_scale * jnp.dot(
        query_low_rank, q_up_local.astype(jnp.float32), precision=lax.Precision.HIGHEST
    )
    keys_new = jnp.dot(normalized_hidden, key_matrix, preferred_element_type=jnp.float32)
    values_new = jnp.dot(
        normalized_hidden, value_matrix, preferred_element_type=jnp.float32
    ).astype(jnp.bfloat16)
    positions = cache_fill_lengths.astype(jnp.float32)
    query_rot = (
        rotate(query_rows.reshape(row_count, local_heads, HEAD_SIZE), positions)
        .astype(jnp.bfloat16)
        .reshape(row_count, local_groups, group_size, HEAD_SIZE)
    )
    key_rot = rotate(keys_new.reshape(row_count, local_groups, HEAD_SIZE), positions).astype(
        jnp.bfloat16
    )
    value_rows = values_new.reshape(row_count, local_groups, HEAD_SIZE)
    score_scale = HEAD_SIZE ** (-0.5)
    scores = (
        jnp.einsum(
            "rkgd,rkcd->rkgc", query_rot, cached_rotated_keys, preferred_element_type=jnp.float32
        )
        * score_scale
    )
    visible = (
        jnp.arange(cache_length, dtype=jnp.int32)[None, None, None, :]
        < cache_fill_lengths[:, None, None, None]
    )
    scores = jnp.where(visible, scores, -jnp.inf)
    own_score = (
        jnp.einsum("rkgd,rkd->rkg", query_rot, key_rot, preferred_element_type=jnp.float32)
        * score_scale
    )
    top_score = jnp.maximum(jnp.max(scores, axis=-1), own_score)
    cache_exp = jnp.exp(scores - top_score[..., None])
    own_exp = jnp.exp(own_score - top_score)
    denominator = jnp.sum(cache_exp, axis=-1) + own_exp
    cache_weight = (cache_exp / denominator[..., None]).astype(jnp.bfloat16)
    own_weight = (own_exp / denominator).astype(jnp.bfloat16)
    attn = jnp.einsum(
        "rkgc,rkcd->rkgd", cache_weight, cached_value_rows, preferred_element_type=jnp.float32
    )
    attn = (
        attn
        + own_weight.astype(jnp.float32)[..., None] * value_rows.astype(jnp.float32)[:, :, None, :]
    )
    attention_flattened = attn.astype(jnp.bfloat16).reshape(row_count, local_heads * HEAD_SIZE)
    low_o_part = jnp.dot(attention_flattened, o_down_local, preferred_element_type=jnp.float32)
    base_contribution = jnp.dot(
        attention_flattened, output_matrix, preferred_element_type=jnp.float32
    )
    output_low_rank = lax.psum(low_o_part, "tp")
    o_up_own = lax.all_gather(output_adapter_up, "dp", axis=1, tiled=True)
    attn_out = lax.psum_scatter(
        base_contribution, "tp", scatter_dimension=1, tiled=True
    ) + adapter_scale * jnp.dot(
        output_low_rank, o_up_own.astype(jnp.float32), precision=lax.Precision.HIGHEST
    )
    return attn_out


def three_parts(values):
    high = values.astype(jnp.bfloat16)
    rest = values - high.astype(jnp.float32)
    middle = rest.astype(jnp.bfloat16)
    low = (rest - middle.astype(jnp.float32)).astype(jnp.bfloat16)
    return jnp.concatenate(
        [high.astype(jnp.float32), middle.astype(jnp.float32), low.astype(jnp.float32)], axis=0
    ).astype(jnp.bfloat16)


def wide_product(parts, right, rows):
    product = jnp.dot(parts, right, preferred_element_type=jnp.float32)
    return product[:rows] + (product[rows : 2 * rows] + product[2 * rows :])


def kernel(
    dp,
    tp,
    x_hbm,
    gain_hbm,
    table_hbm,
    wq_hbm,
    wk_hbm,
    wv_hbm,
    wo_hbm,
    qd_hbm,
    qu_hbm,
    od_hbm,
    ou_hbm,
    k_hbm,
    v_hbm,
    out_ref,
    x_s,
    gain_s,
    table_s,
    wq_s,
    wk_s,
    wv_s,
    wo_s,
    qd_s,
    qu_s,
    od_s,
    ou_s,
    k_s,
    v_s,
    normed_s,
    q_s,
    key_s,
    value_s,
    attn_s,
    low_send,
    low_recv,
    share_send,
    share_recv,
    in_sem,
    w_sem,
    kv_sem,
    wo_sem,
    own_sem,
    gather_send,
    gather_recv,
    low_send_sem,
    low_recv_sem,
    share_send_sem,
    share_recv_sem,
):
    d = lax.axis_index("dp")
    t = lax.axis_index("tp")
    rows, features = x_hbm.shape
    rank = qd_hbm.shape[1]
    groups = k_hbm.shape[1]
    cache = k_hbm.shape[2]
    width = wq_hbm.shape[1]
    heads = width // HEAD_SIZE
    per_group = heads // groups
    pieces = w_sem.shape[1]
    depth = features // pieces
    columns = out_ref.shape[1]
    f32, bf16 = jnp.float32, jnp.bfloat16

    small = [
        pltpu.make_async_copy(src, dst, in_sem.at[i])
        for i, (src, dst) in enumerate(((x_hbm, x_s), (gain_hbm, gain_s), (table_hbm, table_s)))
    ]
    for copy in small:
        copy.start()

    def weight_copies(k):
        span = pl.ds(pl.multiple_of(k * depth, depth), depth)
        return [
            pltpu.make_async_copy(src.at[span], dst.at[span], w_sem.at[i, k])
            for i, (src, dst) in enumerate(((wq_hbm, wq_s), (wk_hbm, wk_s), (wv_hbm, wv_s)))
        ]

    def cache_copies(r):
        return [
            pltpu.make_async_copy(src.at[r], dst.at[r], kv_sem.at[i, r])
            for i, (src, dst) in enumerate(((k_hbm, k_s), (v_hbm, v_s)))
        ]

    def out_copy(step):
        to = lax.rem(t + 1 + step, tp)
        return pltpu.make_async_copy(
            wo_hbm.at[:, pl.ds(pl.multiple_of(to * columns, columns), columns)],
            wo_s.at[step],
            wo_sem.at[step],
        )

    for k in range(pieces):
        for copy in weight_copies(k):
            copy.start()

    factors = ((qd_hbm, qd_s), (qu_hbm, qu_s), (od_hbm, od_s), (ou_hbm, ou_s))
    own = [
        pltpu.make_async_copy(src, dst.at[d], own_sem.at[i]) for i, (src, dst) in enumerate(factors)
    ]
    for copy in own:
        copy.start()

    barrier = pltpu.get_barrier_semaphore()
    for i in range(1, dp):
        pl.semaphore_signal(
            barrier,
            inc=1,
            device_id=(lax.rem(d + i, dp), t),
            device_id_type=pl.DeviceIdType.MESH,
        )
    for i in range(1, tp):
        pl.semaphore_signal(
            barrier,
            inc=1,
            device_id=(d, lax.rem(t + i, tp)),
            device_id_type=pl.DeviceIdType.MESH,
        )

    for copy in small:
        copy.wait()
    hidden = x_s[...].astype(f32)
    normed_s[...] = (
        hidden
        * lax.rsqrt(jnp.mean(hidden * hidden, axis=-1, keepdims=True) + 1e-05)
        * gain_s[...]
    ).astype(bf16)

    pl.semaphore_wait(barrier, dp - 1 + tp - 1)

    def gather(which, i):
        src, dst = factors[which]
        return pltpu.make_async_remote_copy(
            src_ref=src,
            dst_ref=dst.at[d],
            send_sem=gather_send.at[which, i],
            recv_sem=gather_recv.at[which, i],
            device_id=(lax.rem(d + i, dp), t),
            device_id_type=pl.DeviceIdType.MESH,
        )

    def arrived(which, i):
        src, dst = factors[which]
        return pltpu.make_async_remote_copy(
            src_ref=src,
            dst_ref=dst.at[lax.rem(d + dp - i, dp)],
            send_sem=gather_send.at[which, i],
            recv_sem=gather_recv.at[which, i],
            device_id=(lax.rem(d + i, dp), t),
            device_id_type=pl.DeviceIdType.MESH,
        )

    for which in range(len(factors)):
        for i in range(1, dp):
            gather(which, i).start()

    def take(which):
        own[which].wait()
        for i in range(1, dp):
            arrived(which, i).wait_recv()

    def project(k, totals):
        for copy in weight_copies(k):
            copy.wait()
        for copy in cache_copies(k):
            copy.start()
        span = pl.ds(pl.multiple_of(k * depth, depth), depth)
        block = normed_s[:, span]
        return tuple(
            total + jnp.dot(block, weight[span, :], preferred_element_type=f32)
            for total, weight in zip(totals, (wq_s, wk_s, wv_s))
        )

    totals = tuple(jnp.zeros((rows, w.shape[1]), f32) for w in (wq_s, wk_s, wv_s))
    totals = lax.fori_loop(0, pieces // 2, project, totals)

    take(0)
    part_width = qd_hbm.shape[0]
    part = jnp.zeros((rows, rank), f32)
    for i in range(dp):
        at = pl.multiple_of((i * tp + t) * part_width, part_width)
        part += jnp.dot(
            normed_s[:, pl.ds(at, part_width)], qd_s[i], preferred_element_type=f32
        )
    low_send[...] = jnp.concatenate(
        [part, jnp.zeros((rows, HEAD_SIZE - rank), f32)], axis=1
    )

    def low_copy(step):
        return pltpu.make_async_remote_copy(
            src_ref=low_send,
            dst_ref=low_recv.at[step],
            send_sem=low_send_sem.at[step],
            recv_sem=low_recv_sem.at[step],
            device_id=(d, lax.rem(t + 1 + step, tp)),
            device_id_type=pl.DeviceIdType.MESH,
        )

    for step in range(tp - 1):
        low_copy(step).start()

    totals = lax.fori_loop(pieces // 2, pieces, project, totals)
    query_total, key_total, value_total = totals
    for step in range(tp):
        out_copy(step).start()

    cosine = table_s[:, :HEAD_SIZE]
    sine = table_s[:, HEAD_SIZE : 2 * HEAD_SIZE]

    def turned(vectors):
        rolled = pltpu.roll(vectors, HEAD_SIZE // 2, 1)
        return (vectors * cosine + rolled * sine).astype(bf16).astype(f32)

    for g in range(groups):
        span = slice(g * HEAD_SIZE, (g + 1) * HEAD_SIZE)
        key_s[:, g, :] = turned(key_total[:, span])
        value_s[:, g, :] = value_total[:, span].astype(bf16).astype(f32)

    key_s[:, groups, :] = table_s[:, 2 * HEAD_SIZE :]

    take(1)
    low = low_send[...]
    for step in range(tp - 1):
        low_copy(step).wait_recv()
        low += low_recv[step]
    parts = three_parts(low[:, :rank])
    up_width = qu_hbm.shape[1]
    for i in range(dp):
        extra = wide_product(parts, qu_s[i], rows)
        for j in range(up_width // HEAD_SIZE):
            h = i * (up_width // HEAD_SIZE) + j
            base = query_total[:, h * HEAD_SIZE : (h + 1) * HEAD_SIZE]
            q_s[:, h, :] = turned(
                base + adapter_scale * extra[:, j * HEAD_SIZE : (j + 1) * HEAD_SIZE]
            )

    scale = HEAD_SIZE ** (-0.5)
    at_once = 2

    def attend(step, carry):
        for u in range(at_once):
            for copy in cache_copies(step * at_once + u):
                copy.wait()
        place = lax.broadcasted_iota(jnp.int32, (per_group, cache), 1).astype(f32)
        results = []
        for u in range(at_once):
            r = step * at_once + u
            length = key_s[r, groups : groups + 1, :][:, :1]
            for g in range(groups):
                query = q_s[r, g * per_group : (g + 1) * per_group, :]
                scores = (
                    lax.dot_general(
                        query.astype(bf16),
                        k_s[r, g],
                        (((1,), (1,)), ((), ())),
                        preferred_element_type=f32,
                    )
                    * scale
                )
                scores = jnp.where(place < length, scores, -jnp.inf)
                mine = (
                    jnp.sum(query * key_s[r, g : g + 1, :], axis=-1, keepdims=True) * scale
                )
                top = jnp.maximum(jnp.max(scores, axis=-1, keepdims=True), mine)
                powers = jnp.exp(scores - top)
                my_power = jnp.exp(mine - top)
                inverse = 1.0 / (jnp.sum(powers, axis=-1, keepdims=True) + my_power)
                weights = (powers * inverse).astype(bf16)
                my_weight = (my_power * inverse).astype(bf16).astype(f32)
                mixed = jnp.dot(weights, v_s[r, g], preferred_element_type=f32)
                mixed = mixed + my_weight * value_s[r, g : g + 1, :]
                results.append((r, g, mixed.astype(bf16).astype(f32)))
        for r, g, mixed in results:
            attn_s[g * per_group : (g + 1) * per_group, r, :] = mixed
        return carry

    lax.fori_loop(0, rows // at_once, attend, 0)

    flat = jnp.concatenate([attn_s[h] for h in range(heads)], axis=1).astype(bf16)

    take(2)
    down_rows = od_hbm.shape[0]
    low_o = jnp.zeros((rows, rank), f32)
    for i in range(dp):
        low_o += jnp.dot(
            flat[:, i * down_rows : (i + 1) * down_rows], od_s[i], preferred_element_type=f32
        )
    low_o = jnp.concatenate([low_o, jnp.zeros((rows, HEAD_SIZE - rank), f32)], axis=1)

    def share_copy(step):
        return pltpu.make_async_remote_copy(
            src_ref=share_send.at[step],
            dst_ref=share_recv.at[step],
            send_sem=share_send_sem.at[step],
            recv_sem=share_recv_sem.at[step],
            device_id=(d, lax.rem(t + 1 + step, tp)),
            device_id_type=pl.DeviceIdType.MESH,
        )

    tile = 256
    for step in range(tp):
        out_copy(step).wait()

        def columns_of(c, carry, step=step):
            span = pl.ds(pl.multiple_of(c * tile, tile), tile)
            share_send[step, :, span] = jnp.dot(
                flat, wo_s[step, :, span], preferred_element_type=f32
            )
            return carry

        lax.fori_loop(0, columns // tile, columns_of, 0)
        share_send[step, :, columns:] = low_o
        if step < tp - 1:
            share_copy(step).start()

    take(3)
    total = share_send[tp - 1]
    for step in range(tp - 1):
        share_copy(step).wait_recv()
        total += share_recv[step]
    parts = three_parts(total[:, columns : columns + rank])
    last_width = ou_hbm.shape[1]
    for i in range(dp):
        span = slice(i * last_width, (i + 1) * last_width)
        out_ref[:, span] = total[:, span] + adapter_scale * wide_product(parts, ou_s[i], rows)

    for which in range(len(factors)):
        for i in range(1, dp):
            gather(which, i).wait_send()
    for step in range(tp - 1):
        low_copy(step).wait_send()
        share_copy(step).wait_send()


def on_device(
    residual_hidden,
    attention_norm_gain,
    query_matrix,
    key_matrix,
    value_matrix,
    output_matrix,
    query_adapter_down,
    query_adapter_up,
    output_adapter_down,
    output_adapter_up,
    cached_rotated_keys,
    cached_value_rows,
    cache_fill_lengths,
):
    dp, tp = lax.axis_size("dp"), lax.axis_size("tp")
    rows, features = residual_hidden.shape
    rank = query_adapter_down.shape[1]
    width = query_matrix.shape[1]
    heads = width // HEAD_SIZE
    groups = key_matrix.shape[1] // HEAD_SIZE
    columns = output_matrix.shape[1] // tp
    half = HEAD_SIZE // 2
    lengths = cache_fill_lengths.astype(jnp.float32)[:, None]
    inverse = jnp.exp(
        jnp.arange(half, dtype=jnp.float32) * (-2.0 * math.log(rope_theta) / HEAD_SIZE)
    )
    angles = lengths * inverse[None, :]
    cosine, sine = jnp.cos(angles), jnp.sin(angles)
    table = jnp.concatenate(
        [cosine, cosine, -sine, sine, jnp.broadcast_to(lengths, (rows, HEAD_SIZE))], axis=1
    )
    pieces = rows
    bf16, f32 = jnp.bfloat16, jnp.float32
    operands = (
        residual_hidden,
        attention_norm_gain.reshape(1, features),
        table,
        query_matrix,
        key_matrix,
        value_matrix,
        output_matrix,
        query_adapter_down,
        query_adapter_up,
        output_adapter_down,
        output_adapter_up,
        cached_rotated_keys,
        cached_value_rows,
    )
    return pl.pallas_call(
        functools.partial(kernel, dp, tp),
        out_shape=jax.ShapeDtypeStruct((rows, columns), f32),
        in_specs=[pl.BlockSpec(memory_space=pl.ANY)] * len(operands),
        out_specs=pl.BlockSpec(memory_space=pltpu.VMEM),
        scratch_shapes=[
            pltpu.VMEM(residual_hidden.shape, bf16),
            pltpu.VMEM((1, features), f32),
            pltpu.VMEM(table.shape, f32),
            pltpu.VMEM(query_matrix.shape, bf16),
            pltpu.VMEM(key_matrix.shape, bf16),
            pltpu.VMEM(value_matrix.shape, bf16),
            pltpu.VMEM((tp, width, columns), bf16),
            pltpu.VMEM((dp,) + query_adapter_down.shape, bf16),
            pltpu.VMEM((dp,) + query_adapter_up.shape, bf16),
            pltpu.VMEM((dp,) + output_adapter_down.shape, bf16),
            pltpu.VMEM((dp,) + output_adapter_up.shape, bf16),
            pltpu.VMEM(cached_rotated_keys.shape, bf16),
            pltpu.VMEM(cached_value_rows.shape, bf16),
            pltpu.VMEM((rows, features), bf16),
            pltpu.VMEM((rows, heads, HEAD_SIZE), f32),
            pltpu.VMEM((rows, groups + 1, HEAD_SIZE), f32),
            pltpu.VMEM((rows, groups, HEAD_SIZE), f32),
            pltpu.VMEM((heads, rows, HEAD_SIZE), f32),
            pltpu.VMEM((rows, HEAD_SIZE), f32),
            pltpu.VMEM((tp - 1, rows, HEAD_SIZE), f32),
            pltpu.VMEM((tp, rows, columns + HEAD_SIZE), f32),
            pltpu.VMEM((tp - 1, rows, columns + HEAD_SIZE), f32),
            pltpu.SemaphoreType.DMA((3,)),
            pltpu.SemaphoreType.DMA((3, pieces)),
            pltpu.SemaphoreType.DMA((2, rows)),
            pltpu.SemaphoreType.DMA((tp,)),
            pltpu.SemaphoreType.DMA((4,)),
            pltpu.SemaphoreType.DMA((4, dp)),
            pltpu.SemaphoreType.DMA((4, dp)),
            pltpu.SemaphoreType.DMA((tp - 1,)),
            pltpu.SemaphoreType.DMA((tp - 1,)),
            pltpu.SemaphoreType.DMA((tp - 1,)),
            pltpu.SemaphoreType.DMA((tp - 1,)),
        ],
        compiler_params=pltpu.CompilerParams(
            collective_id=0, has_side_effects=True, vmem_limit_bytes=56 * 1024 * 1024
        ),
    )(*operands)


def solution(mesh):
    in_specs = (
        P("dp", None),
        P(),
        P(None, "tp"),
        P(None, "tp"),
        P(None, "tp"),
        P("tp", None),
        P(("dp", "tp"), None),
        P(None, ("tp", "dp")),
        P(("tp", "dp"), None),
        P(None, ("tp", "dp")),
        P("dp", "tp", None, None),
        P("dp", "tp", None, None),
        P("dp"),
    )
    out_specs = P("dp", "tp")

    def local(*arrays):
        wide = arrays[7].shape[1] % HEAD_SIZE == 0 and arrays[9].shape[1] % HEAD_SIZE == 0
        return (on_device if wide else on_device_narrow)(*arrays)

    return jax.shard_map(
        local, mesh=mesh, in_specs=in_specs, out_specs=out_specs, check_vma=False
    )
```

```python
import functools
import math

import jax
import jax.numpy as jnp
from jax import lax
from jax.experimental import pallas as pl
from jax.experimental.pallas import tpu as pltpu
from jax.sharding import PartitionSpec as P

HEAD_SIZE = 128


adapter_scale = 2.0
rope_theta = 500000.0


def rotate(vectors, positions):
    half_dim = vectors.shape[-1] // 2
    steps_idx = jnp.arange(half_dim, dtype=jnp.float32)
    inverse = jnp.exp(steps_idx * (-2.0 * math.log(rope_theta) / vectors.shape[-1]))
    angles = positions[:, None, None] * inverse[None, None, :]
    cosine = jnp.cos(angles)
    sine = jnp.sin(angles)
    first = vectors[..., :half_dim]
    second = vectors[..., half_dim:]
    return jnp.concatenate(
        [first * cosine - second * sine, second * cosine + first * sine], axis=-1
    )


def on_device_narrow(
    residual_hidden,
    attention_norm_gain,
    query_matrix,
    key_matrix,
    value_matrix,
    output_matrix,
    query_adapter_down,
    query_adapter_up,
    output_adapter_down,
    output_adapter_up,
    cached_rotated_keys,
    cached_value_rows,
    cache_fill_lengths,
):
    row_count = residual_hidden.shape[0]
    feature_width = residual_hidden.shape[1]
    rank_width = query_adapter_down.shape[1]
    local_heads = query_matrix.shape[1] // HEAD_SIZE
    local_groups = key_matrix.shape[1] // HEAD_SIZE
    group_size = local_heads // local_groups
    cache_length = cached_rotated_keys.shape[2]
    hidden_f = residual_hidden.astype(jnp.float32)
    normalized_hidden = (
        hidden_f
        * lax.rsqrt(jnp.mean(hidden_f * hidden_f, axis=-1, keepdims=True) + 1e-05)
        * attention_norm_gain
    ).astype(jnp.bfloat16)
    q_up_local, o_down_local = (
        lax.all_gather(query_adapter_up, "dp", axis=1, tiled=True),
        lax.all_gather(output_adapter_down, "dp", axis=0, tiled=True),
    )
    q_down_share = lax.all_gather(query_adapter_down, "dp", axis=0, tiled=True)
    dp_count = lax.axis_size("dp")
    tp_count = lax.axis_size("tp")
    block_width = feature_width // (dp_count * tp_count)
    picked = lax.dynamic_index_in_dim(
        normalized_hidden.reshape(row_count, dp_count, tp_count, block_width),
        lax.axis_index("tp"),
        2,
        keepdims=False,
    )
    partial_low = jnp.einsum(
        "rdb,dbk->rk",
        picked,
        q_down_share.reshape(dp_count, block_width, rank_width),
        preferred_element_type=jnp.float32,
    )
    query_low_rank = lax.psum(partial_low, "tp")
    query_rows = jnp.dot(
        normalized_hidden, query_matrix, preferred_element_type=jnp.float32
    ) + adapter_scale * jnp.dot(
        query_low_rank, q_up_local.astype(jnp.float32), precision=lax.Precision.HIGHEST
    )
    keys_new = jnp.dot(normalized_hidden, key_matrix, preferred_element_type=jnp.float32)
    values_new = jnp.dot(
        normalized_hidden, value_matrix, preferred_element_type=jnp.float32
    ).astype(jnp.bfloat16)
    positions = cache_fill_lengths.astype(jnp.float32)
    query_rot = (
        rotate(query_rows.reshape(row_count, local_heads, HEAD_SIZE), positions)
        .astype(jnp.bfloat16)
        .reshape(row_count, local_groups, group_size, HEAD_SIZE)
    )
    key_rot = rotate(keys_new.reshape(row_count, local_groups, HEAD_SIZE), positions).astype(
        jnp.bfloat16
    )
    value_rows = values_new.reshape(row_count, local_groups, HEAD_SIZE)
    score_scale = HEAD_SIZE ** (-0.5)
    scores = (
        jnp.einsum(
            "rkgd,rkcd->rkgc", query_rot, cached_rotated_keys, preferred_element_type=jnp.float32
        )
        * score_scale
    )
    visible = (
        jnp.arange(cache_length, dtype=jnp.int32)[None, None, None, :]
        < cache_fill_lengths[:, None, None, None]
    )
    scores = jnp.where(visible, scores, -jnp.inf)
    own_score = (
        jnp.einsum("rkgd,rkd->rkg", query_rot, key_rot, preferred_element_type=jnp.float32)
        * score_scale
    )
    top_score = jnp.maximum(jnp.max(scores, axis=-1), own_score)
    cache_exp = jnp.exp(scores - top_score[..., None])
    own_exp = jnp.exp(own_score - top_score)
    denominator = jnp.sum(cache_exp, axis=-1) + own_exp
    cache_weight = (cache_exp / denominator[..., None]).astype(jnp.bfloat16)
    own_weight = (own_exp / denominator).astype(jnp.bfloat16)
    attn = jnp.einsum(
        "rkgc,rkcd->rkgd", cache_weight, cached_value_rows, preferred_element_type=jnp.float32
    )
    attn = (
        attn
        + own_weight.astype(jnp.float32)[..., None] * value_rows.astype(jnp.float32)[:, :, None, :]
    )
    attention_flattened = attn.astype(jnp.bfloat16).reshape(row_count, local_heads * HEAD_SIZE)
    low_o_part = jnp.dot(attention_flattened, o_down_local, preferred_element_type=jnp.float32)
    base_contribution = jnp.dot(
        attention_flattened, output_matrix, preferred_element_type=jnp.float32
    )
    output_low_rank = lax.psum(low_o_part, "tp")
    o_up_own = lax.all_gather(output_adapter_up, "dp", axis=1, tiled=True)
    attn_out = lax.psum_scatter(
        base_contribution, "tp", scatter_dimension=1, tiled=True
    ) + adapter_scale * jnp.dot(
        output_low_rank, o_up_own.astype(jnp.float32), precision=lax.Precision.HIGHEST
    )
    return attn_out


def three_parts(values):
    high = values.astype(jnp.bfloat16)
    rest = values - high.astype(jnp.float32)
    middle = rest.astype(jnp.bfloat16)
    low = (rest - middle.astype(jnp.float32)).astype(jnp.bfloat16)
    return jnp.concatenate(
        [high.astype(jnp.float32), middle.astype(jnp.float32), low.astype(jnp.float32)], axis=0
    ).astype(jnp.bfloat16)


def wide_product(parts, right, rows):
    product = jnp.dot(parts, right, preferred_element_type=jnp.float32)
    return product[:rows] + (product[rows : 2 * rows] + product[2 * rows :])


def kernel(
    dp,
    tp,
    x_hbm,
    gain_hbm,
    lengths_hbm,
    wq_hbm,
    wk_hbm,
    wv_hbm,
    wo_hbm,
    qd_hbm,
    qu_hbm,
    od_hbm,
    ou_hbm,
    k_hbm,
    v_hbm,
    base_ref,
    extra_ref,
    x_s,
    gain_s,
    lengths_s,
    table_s,
    wq_s,
    wk_s,
    wv_s,
    wo_s,
    qd_s,
    qu_s,
    od_s,
    ou_s,
    k_s,
    v_s,
    normed_s,
    q_s,
    key_s,
    value_s,
    attn_s,
    low_send,
    low_recv,
    share_send,
    share_recv,
    in_sem,
    w_sem,
    kv_sem,
    wo_sem,
    own_sem,
    gather_send,
    gather_recv,
    relay_send,
    relay_recv,
    low_send_sem,
    low_recv_sem,
    share_send_sem,
    share_recv_sem,
):
    d = lax.axis_index("dp")
    t = lax.axis_index("tp")
    rows, features = x_hbm.shape
    rank = qd_hbm.shape[0]
    groups = k_hbm.shape[1]
    cache = k_hbm.shape[2]
    width = wq_hbm.shape[1]
    heads = width // HEAD_SIZE
    per_group = heads // groups
    pieces = w_sem.shape[1]
    depth = features // pieces
    columns = base_ref.shape[1]
    f32, bf16 = jnp.float32, jnp.bfloat16

    small = [
        pltpu.make_async_copy(src, dst, in_sem.at[i])
        for i, (src, dst) in enumerate(((x_hbm, x_s), (gain_hbm, gain_s), (lengths_hbm, lengths_s)))
    ]
    for copy in small:
        copy.start()

    def weight_copies(k):
        span = pl.ds(pl.multiple_of(k * depth, depth), depth)
        return [
            pltpu.make_async_copy(src.at[span], dst.at[span], w_sem.at[i, k])
            for i, (src, dst) in enumerate(((wq_hbm, wq_s), (wk_hbm, wk_s), (wv_hbm, wv_s)))
        ]

    def cache_copies(r):
        return [
            pltpu.make_async_copy(src.at[r], dst.at[r], kv_sem.at[i, r])
            for i, (src, dst) in enumerate(((k_hbm, k_s), (v_hbm, v_s)))
        ]

    halves = wo_sem.shape[1]
    half_rows = width // halves

    def out_copy(step, half):
        to = lax.rem(t + 1 + step, tp)
        span = pl.ds(pl.multiple_of(half * half_rows, half_rows), half_rows)
        return pltpu.make_async_copy(
            wo_hbm.at[span, pl.ds(pl.multiple_of(to * columns, columns), columns)],
            wo_s.at[step, span],
            wo_sem.at[step, half],
        )

    ahead = pieces // 2
    for k in range(ahead):
        for copy in weight_copies(k):
            copy.start()

    factors = ((qd_hbm, qd_s), (qu_hbm, qu_s), (od_hbm, od_s), (ou_hbm, ou_s))
    own = [
        pltpu.make_async_copy(src, dst.at[d], own_sem.at[i]) for i, (src, dst) in enumerate(factors)
    ]
    for copy in own:
        copy.start()

    chips = dp // 2
    sibling = d + 1 - 2 * lax.rem(d, 2)

    def same_core(i):
        return lax.rem(d + 2 * i, dp)

    barrier = pltpu.get_barrier_semaphore()
    peers = [(same_core(i), t) for i in range(1, chips)] + [(sibling, t)]
    peers += [(d, lax.rem(t + i, tp)) for i in range(1, tp)]
    for peer in peers:
        pl.semaphore_signal(
            barrier, inc=1, device_id=peer, device_id_type=pl.DeviceIdType.MESH
        )

    for copy in small:
        copy.wait()
    hidden = x_s[...].astype(f32)
    normed_s[...] = (
        hidden
        * lax.rsqrt(jnp.mean(hidden * hidden, axis=-1, keepdims=True) + 1e-05)
        * gain_s[...]
    ).astype(bf16)

    lengths = jnp.sum(
        jnp.where(
            lax.broadcasted_iota(jnp.int32, (rows, rows), 0)
            == lax.broadcasted_iota(jnp.int32, (rows, rows), 1),
            jnp.broadcast_to(lengths_s[...].astype(f32), (rows, rows)),
            0.0,
        ),
        axis=1,
        keepdims=True,
    )
    lane = lax.broadcasted_iota(jnp.int32, (rows, HEAD_SIZE), 1)
    first = lane < HEAD_SIZE // 2
    number = jnp.where(first, lane, lane - HEAD_SIZE // 2).astype(f32)
    angles = lengths * jnp.exp(number * (-2.0 * math.log(rope_theta) / HEAD_SIZE))
    table_s[:, :HEAD_SIZE] = jnp.cos(angles)
    table_s[:, HEAD_SIZE:] = jnp.where(first, -jnp.sin(angles), jnp.sin(angles))
    key_s[:, groups, :] = jnp.broadcast_to(lengths, (rows, HEAD_SIZE))

    pl.semaphore_wait(barrier, len(peers))

    def gather(which, i):
        src, dst = factors[which]
        return pltpu.make_async_remote_copy(
            src_ref=src,
            dst_ref=dst.at[d],
            send_sem=gather_send.at[which, i],
            recv_sem=gather_recv.at[which, i],
            device_id=(same_core(i), t),
            device_id_type=pl.DeviceIdType.MESH,
        )

    def relayed(which, i, core):
        dst = factors[which][1]
        slot = lax.rem(core + dp - 2 * i, dp)
        return pltpu.make_async_remote_copy(
            src_ref=dst.at[slot] if i else factors[which][0],
            dst_ref=dst.at[slot],
            send_sem=relay_send.at[which, i],
            recv_sem=relay_recv.at[which, i],
            device_id=(sibling, t),
            device_id_type=pl.DeviceIdType.MESH,
        )

    def arrived(which, i):
        src, dst = factors[which]
        return pltpu.make_async_remote_copy(
            src_ref=src,
            dst_ref=dst.at[lax.rem(d + dp - 2 * i, dp)],
            send_sem=gather_send.at[which, i],
            recv_sem=gather_recv.at[which, i],
            device_id=(same_core(i), t),
            device_id_type=pl.DeviceIdType.MESH,
        )

    def spread(which):
        for i in range(1, chips):
            gather(which, i).start()
        relayed(which, 0, d).start()

    def relay(which):
        for i in range(1, chips):
            arrived(which, i).wait_recv()
            relayed(which, i, d).start()

    def take(which):
        own[which].wait()
        for i in range(chips):
            relayed(which, i, sibling).wait_recv()

    spread(0)
    spread(1)

    def project(k, totals):
        for copy in weight_copies(k):
            copy.wait()

        @pl.when(k < pieces - ahead)
        def _():
            for copy in weight_copies(k + ahead):
                copy.start()

        @pl.when(k >= pieces - ahead)
        def _():
            for u in range(2):
                for copy in cache_copies((k - (pieces - ahead)) * 2 + u):
                    copy.start()

        span = pl.ds(pl.multiple_of(k * depth, depth), depth)
        block = normed_s[:, span]
        return tuple(
            total + jnp.dot(block, weight[span, :], preferred_element_type=f32)
            for total, weight in zip(totals, (wq_s, wk_s, wv_s))
        )

    totals = tuple(jnp.zeros((rows, w.shape[1]), f32) for w in (wq_s, wk_s, wv_s))
    totals = lax.fori_loop(0, pieces // 2, project, totals)

    relay(0)
    relay(1)
    take(0)
    part_width = qd_hbm.shape[1]
    part = jnp.zeros((rows, rank), f32)
    for i in range(dp):
        at = pl.multiple_of((i * tp + t) * part_width, part_width)
        part += lax.dot_general(
            normed_s[:, pl.ds(at, part_width)],
            qd_s[i],
            (((1,), (1,)), ((), ())),
            preferred_element_type=f32,
        )
    low_send[...] = jnp.concatenate(
        [part, jnp.zeros((rows, HEAD_SIZE - rank), f32)], axis=1
    )

    def low_copy(step):
        return pltpu.make_async_remote_copy(
            src_ref=low_send,
            dst_ref=low_recv.at[step],
            send_sem=low_send_sem.at[step],
            recv_sem=low_recv_sem.at[step],
            device_id=(d, lax.rem(t + 1 + step, tp)),
            device_id_type=pl.DeviceIdType.MESH,
        )

    for step in range(tp - 1):
        low_copy(step).start()

    totals = lax.fori_loop(pieces // 2, pieces, project, totals)
    query_total, key_total, value_total = totals
    cosine = table_s[:, :HEAD_SIZE]
    sine = table_s[:, HEAD_SIZE:]

    def turned(vectors):
        rolled = pltpu.roll(vectors, HEAD_SIZE // 2, 1)
        return (vectors * cosine + rolled * sine).astype(bf16).astype(f32)

    for g in range(groups):
        span = slice(g * HEAD_SIZE, (g + 1) * HEAD_SIZE)
        key_s[:, g, :] = turned(key_total[:, span])
        value_s[:, g, :] = value_total[:, span].astype(bf16).astype(f32)

    spread(2)
    spread(3)
    take(1)
    low = low_send[...]
    for step in range(tp - 1):
        low_copy(step).wait_recv()
        low += low_recv[step]
    parts = three_parts(low[:, :rank])
    up_width = qu_hbm.shape[1]
    for i in range(dp):
        extra = wide_product(parts, qu_s[i], rows)
        for j in range(up_width // HEAD_SIZE):
            h = i * (up_width // HEAD_SIZE) + j
            base = query_total[:, h * HEAD_SIZE : (h + 1) * HEAD_SIZE]
            q_s[:, h, :] = turned(
                base + adapter_scale * extra[:, j * HEAD_SIZE : (j + 1) * HEAD_SIZE]
            )

    scale = HEAD_SIZE ** (-0.5)
    at_once = 2
    units_each = tp * halves * at_once // rows

    def attend(step, carry):
        for u in range(at_once):
            for copy in cache_copies(step * at_once + u):
                copy.wait()
        for u in range(units_each):
            unit = step * units_each + u
            out_copy(unit // halves, unit % halves).start()
        place = lax.broadcasted_iota(jnp.int32, (per_group, cache), 1).astype(f32)
        results = []
        for u in range(at_once):
            r = step * at_once + u
            length = key_s[r, groups : groups + 1, :][:, :1]
            for g in range(groups):
                query = q_s[r, g * per_group : (g + 1) * per_group, :]
                scores = (
                    lax.dot_general(
                        query.astype(bf16),
                        k_s[r, g],
                        (((1,), (1,)), ((), ())),
                        preferred_element_type=f32,
                    )
                    * scale
                )
                scores = jnp.where(place < length, scores, -jnp.inf)
                mine = (
                    jnp.sum(query * key_s[r, g : g + 1, :], axis=-1, keepdims=True) * scale
                )
                top = jnp.maximum(jnp.max(scores, axis=-1, keepdims=True), mine)
                powers = jnp.exp(scores - top)
                my_power = jnp.exp(mine - top)
                inverse = 1.0 / (jnp.sum(powers, axis=-1, keepdims=True) + my_power)
                weights = (powers * inverse).astype(bf16)
                my_weight = (my_power * inverse).astype(bf16).astype(f32)
                mixed = jnp.dot(weights, v_s[r, g], preferred_element_type=f32)
                mixed = mixed + my_weight * value_s[r, g : g + 1, :]
                results.append((r, g, mixed.astype(bf16).astype(f32)))
        for r, g, mixed in results:
            attn_s[g * per_group : (g + 1) * per_group, r, :] = mixed
        return carry

    lax.fori_loop(0, rows // at_once // 2, attend, 0)
    relay(2)
    relay(3)
    lax.fori_loop(rows // at_once // 2, rows // at_once, attend, 0)

    flat = jnp.concatenate([attn_s[h] for h in range(heads)], axis=1).astype(bf16)

    take(2)
    down_rows = od_hbm.shape[1]
    low_o = jnp.zeros((rows, rank), f32)
    for i in range(dp):
        low_o += lax.dot_general(
            flat[:, i * down_rows : (i + 1) * down_rows],
            od_s[i],
            (((1,), (1,)), ((), ())),
            preferred_element_type=f32,
        )
    low_o = jnp.concatenate([low_o, jnp.zeros((rows, HEAD_SIZE - rank), f32)], axis=1)

    def share_copy(step):
        return pltpu.make_async_remote_copy(
            src_ref=share_send.at[step],
            dst_ref=share_recv.at[step],
            send_sem=share_send_sem.at[step],
            recv_sem=share_recv_sem.at[step],
            device_id=(d, lax.rem(t + 1 + step, tp)),
            device_id_type=pl.DeviceIdType.MESH,
        )

    tile = 256
    for step in range(tp):
        for half in range(halves):
            out_copy(step, half).wait()

        def columns_of(c, carry, step=step):
            span = pl.ds(pl.multiple_of(c * tile, tile), tile)
            share_send[step, :, span] = jnp.dot(
                flat, wo_s[step, :, span], preferred_element_type=f32
            )
            return carry

        lax.fori_loop(0, columns // tile, columns_of, 0)
        share_send[step, :, columns:] = low_o
        if step < tp - 1:
            share_copy(step).start()

    take(3)
    total = share_send[tp - 1]
    for step in range(tp - 1):
        share_copy(step).wait_recv()
        total += share_recv[step]
    parts = three_parts(total[:, columns : columns + rank])
    last_width = ou_hbm.shape[1]
    for i in range(dp):
        span = slice(i * last_width, (i + 1) * last_width)
        extra_ref[:, span] = adapter_scale * wide_product(parts, ou_s[i], rows)
    base_ref[...] = total[:, :columns]

    for which in range(len(factors)):
        for i in range(1, chips):
            gather(which, i).wait_send()
        for i in range(chips):
            relayed(which, i, d).wait_send()
    for step in range(tp - 1):
        low_copy(step).wait_send()
        share_copy(step).wait_send()


def on_device(
    residual_hidden,
    attention_norm_gain,
    query_matrix,
    key_matrix,
    value_matrix,
    output_matrix,
    query_adapter_down,
    query_adapter_up,
    output_adapter_down,
    output_adapter_up,
    cached_rotated_keys,
    cached_value_rows,
    cache_fill_lengths,
):
    dp, tp = lax.axis_size("dp"), lax.axis_size("tp")
    rows, features = residual_hidden.shape
    width = query_matrix.shape[1]
    heads = width // HEAD_SIZE
    groups = key_matrix.shape[1] // HEAD_SIZE
    columns = output_matrix.shape[1] // tp
    pieces = rows
    bf16, f32 = jnp.bfloat16, jnp.float32
    operands = (
        residual_hidden,
        attention_norm_gain.reshape(1, features),
        cache_fill_lengths.reshape(1, rows),
        query_matrix,
        key_matrix,
        value_matrix,
        output_matrix,
        query_adapter_down.T,
        query_adapter_up,
        output_adapter_down.T,
        output_adapter_up,
        cached_rotated_keys,
        cached_value_rows,
    )
    base, extra = pl.pallas_call(
        functools.partial(kernel, dp, tp),
        out_shape=[jax.ShapeDtypeStruct((rows, columns), f32)] * 2,
        in_specs=[pl.BlockSpec(memory_space=pl.ANY)] * len(operands),
        out_specs=[pl.BlockSpec(memory_space=pltpu.VMEM)] * 2,
        scratch_shapes=[
            pltpu.VMEM(residual_hidden.shape, bf16),
            pltpu.VMEM((1, features), f32),
            pltpu.VMEM((1, rows), jnp.int32),
            pltpu.VMEM((rows, 2 * HEAD_SIZE), f32),
            pltpu.VMEM(query_matrix.shape, bf16),
            pltpu.VMEM(key_matrix.shape, bf16),
            pltpu.VMEM(value_matrix.shape, bf16),
            pltpu.VMEM((tp, width, columns), bf16),
            pltpu.VMEM((dp,) + query_adapter_down.shape[::-1], bf16),
            pltpu.VMEM((dp,) + query_adapter_up.shape, bf16),
            pltpu.VMEM((dp,) + output_adapter_down.shape[::-1], bf16),
            pltpu.VMEM((dp,) + output_adapter_up.shape, bf16),
            pltpu.VMEM(cached_rotated_keys.shape, bf16),
            pltpu.VMEM(cached_value_rows.shape, bf16),
            pltpu.VMEM((rows, features), bf16),
            pltpu.VMEM((rows, heads, HEAD_SIZE), f32),
            pltpu.VMEM((rows, groups + 1, HEAD_SIZE), f32),
            pltpu.VMEM((rows, groups, HEAD_SIZE), f32),
            pltpu.VMEM((heads, rows, HEAD_SIZE), f32),
            pltpu.VMEM((rows, HEAD_SIZE), f32),
            pltpu.VMEM((tp - 1, rows, HEAD_SIZE), f32),
            pltpu.VMEM((tp, rows, columns + HEAD_SIZE), f32),
            pltpu.VMEM((tp - 1, rows, columns + HEAD_SIZE), f32),
            pltpu.SemaphoreType.DMA((3,)),
            pltpu.SemaphoreType.DMA((3, pieces)),
            pltpu.SemaphoreType.DMA((2, rows)),
            pltpu.SemaphoreType.DMA((tp, 2)),
            pltpu.SemaphoreType.DMA((4,)),
            pltpu.SemaphoreType.DMA((4, dp // 2)),
            pltpu.SemaphoreType.DMA((4, dp // 2)),
            pltpu.SemaphoreType.DMA((4, dp // 2)),
            pltpu.SemaphoreType.DMA((4, dp // 2)),
            pltpu.SemaphoreType.DMA((tp - 1,)),
            pltpu.SemaphoreType.DMA((tp - 1,)),
            pltpu.SemaphoreType.DMA((tp - 1,)),
            pltpu.SemaphoreType.DMA((tp - 1,)),
        ],
        compiler_params=pltpu.CompilerParams(
            collective_id=0, has_side_effects=True, vmem_limit_bytes=56 * 1024 * 1024
        ),
    )(*operands)
    return base + extra


def solution(mesh):
    in_specs = (
        P("dp", None),
        P(),
        P(None, "tp"),
        P(None, "tp"),
        P(None, "tp"),
        P("tp", None),
        P(("dp", "tp"), None),
        P(None, ("tp", "dp")),
        P(("tp", "dp"), None),
        P(None, ("tp", "dp")),
        P("dp", "tp", None, None),
        P("dp", "tp", None, None),
        P("dp"),
    )
    out_specs = P("dp", "tp")

    def local(*arrays):
        wide = arrays[7].shape[1] % HEAD_SIZE == 0 and arrays[9].shape[1] % HEAD_SIZE == 0
        return (on_device if wide else on_device_narrow)(*arrays)

    return jax.shard_map(
        local, mesh=mesh, in_specs=in_specs, out_specs=out_specs, check_vma=False
    )
```

```python
import functools
import math

import jax
import jax.numpy as jnp
from jax import lax
from jax.experimental import pallas as pl
from jax.experimental.pallas import tpu as pltpu
from jax.sharding import PartitionSpec as P

HEAD_SIZE = 128


adapter_scale = 2.0
rope_theta = 500000.0


def rotate(vectors, positions):
    half_dim = vectors.shape[-1] // 2
    steps_idx = jnp.arange(half_dim, dtype=jnp.float32)
    inverse = jnp.exp(steps_idx * (-2.0 * math.log(rope_theta) / vectors.shape[-1]))
    angles = positions[:, None, None] * inverse[None, None, :]
    cosine = jnp.cos(angles)
    sine = jnp.sin(angles)
    first = vectors[..., :half_dim]
    second = vectors[..., half_dim:]
    return jnp.concatenate(
        [first * cosine - second * sine, second * cosine + first * sine], axis=-1
    )


def on_device_narrow(
    residual_hidden,
    attention_norm_gain,
    query_matrix,
    key_matrix,
    value_matrix,
    output_matrix,
    query_adapter_down,
    query_adapter_up,
    output_adapter_down,
    output_adapter_up,
    cached_rotated_keys,
    cached_value_rows,
    cache_fill_lengths,
):
    row_count = residual_hidden.shape[0]
    feature_width = residual_hidden.shape[1]
    rank_width = query_adapter_down.shape[1]
    local_heads = query_matrix.shape[1] // HEAD_SIZE
    local_groups = key_matrix.shape[1] // HEAD_SIZE
    group_size = local_heads // local_groups
    cache_length = cached_rotated_keys.shape[2]
    hidden_f = residual_hidden.astype(jnp.float32)
    normalized_hidden = (
        hidden_f
        * lax.rsqrt(jnp.mean(hidden_f * hidden_f, axis=-1, keepdims=True) + 1e-05)
        * attention_norm_gain
    ).astype(jnp.bfloat16)
    q_up_local, o_down_local = (
        lax.all_gather(query_adapter_up, "dp", axis=1, tiled=True),
        lax.all_gather(output_adapter_down, "dp", axis=0, tiled=True),
    )
    q_down_share = lax.all_gather(query_adapter_down, "dp", axis=0, tiled=True)
    dp_count = lax.axis_size("dp")
    tp_count = lax.axis_size("tp")
    block_width = feature_width // (dp_count * tp_count)
    picked = lax.dynamic_index_in_dim(
        normalized_hidden.reshape(row_count, dp_count, tp_count, block_width),
        lax.axis_index("tp"),
        2,
        keepdims=False,
    )
    partial_low = jnp.einsum(
        "rdb,dbk->rk",
        picked,
        q_down_share.reshape(dp_count, block_width, rank_width),
        preferred_element_type=jnp.float32,
    )
    query_low_rank = lax.psum(partial_low, "tp")
    query_rows = jnp.dot(
        normalized_hidden, query_matrix, preferred_element_type=jnp.float32
    ) + adapter_scale * jnp.dot(
        query_low_rank, q_up_local.astype(jnp.float32), precision=lax.Precision.HIGHEST
    )
    keys_new = jnp.dot(normalized_hidden, key_matrix, preferred_element_type=jnp.float32)
    values_new = jnp.dot(
        normalized_hidden, value_matrix, preferred_element_type=jnp.float32
    ).astype(jnp.bfloat16)
    positions = cache_fill_lengths.astype(jnp.float32)
    query_rot = (
        rotate(query_rows.reshape(row_count, local_heads, HEAD_SIZE), positions)
        .astype(jnp.bfloat16)
        .reshape(row_count, local_groups, group_size, HEAD_SIZE)
    )
    key_rot = rotate(keys_new.reshape(row_count, local_groups, HEAD_SIZE), positions).astype(
        jnp.bfloat16
    )
    value_rows = values_new.reshape(row_count, local_groups, HEAD_SIZE)
    score_scale = HEAD_SIZE ** (-0.5)
    scores = (
        jnp.einsum(
            "rkgd,rkcd->rkgc", query_rot, cached_rotated_keys, preferred_element_type=jnp.float32
        )
        * score_scale
    )
    visible = (
        jnp.arange(cache_length, dtype=jnp.int32)[None, None, None, :]
        < cache_fill_lengths[:, None, None, None]
    )
    scores = jnp.where(visible, scores, -jnp.inf)
    own_score = (
        jnp.einsum("rkgd,rkd->rkg", query_rot, key_rot, preferred_element_type=jnp.float32)
        * score_scale
    )
    top_score = jnp.maximum(jnp.max(scores, axis=-1), own_score)
    cache_exp = jnp.exp(scores - top_score[..., None])
    own_exp = jnp.exp(own_score - top_score)
    denominator = jnp.sum(cache_exp, axis=-1) + own_exp
    cache_weight = (cache_exp / denominator[..., None]).astype(jnp.bfloat16)
    own_weight = (own_exp / denominator).astype(jnp.bfloat16)
    attn = jnp.einsum(
        "rkgc,rkcd->rkgd", cache_weight, cached_value_rows, preferred_element_type=jnp.float32
    )
    attn = (
        attn
        + own_weight.astype(jnp.float32)[..., None] * value_rows.astype(jnp.float32)[:, :, None, :]
    )
    attention_flattened = attn.astype(jnp.bfloat16).reshape(row_count, local_heads * HEAD_SIZE)
    low_o_part = jnp.dot(attention_flattened, o_down_local, preferred_element_type=jnp.float32)
    base_contribution = jnp.dot(
        attention_flattened, output_matrix, preferred_element_type=jnp.float32
    )
    output_low_rank = lax.psum(low_o_part, "tp")
    o_up_own = lax.all_gather(output_adapter_up, "dp", axis=1, tiled=True)
    attn_out = lax.psum_scatter(
        base_contribution, "tp", scatter_dimension=1, tiled=True
    ) + adapter_scale * jnp.dot(
        output_low_rank, o_up_own.astype(jnp.float32), precision=lax.Precision.HIGHEST
    )
    return attn_out


def three_parts(values):
    high = values.astype(jnp.bfloat16)
    rest = values - high.astype(jnp.float32)
    middle = rest.astype(jnp.bfloat16)
    low = (rest - middle.astype(jnp.float32)).astype(jnp.bfloat16)
    return jnp.concatenate(
        [high.astype(jnp.float32), middle.astype(jnp.float32), low.astype(jnp.float32)], axis=0
    ).astype(jnp.bfloat16)


def wide_product(parts, right, rows):
    product = jnp.dot(parts, right, preferred_element_type=jnp.float32)
    return product[:rows] + (product[rows : 2 * rows] + product[2 * rows :])


def kernel(
    dp,
    tp,
    x_hbm,
    gain_hbm,
    lengths_hbm,
    wq_hbm,
    wk_hbm,
    wv_hbm,
    wo_hbm,
    qd_hbm,
    qu_hbm,
    od_hbm,
    ou_hbm,
    k_hbm,
    v_hbm,
    base_ref,
    extra_ref,
    x_s,
    gain_s,
    lengths_s,
    table_s,
    wq_s,
    wk_s,
    wv_s,
    wo_s,
    qd_s,
    qu_s,
    od_s,
    ou_s,
    k_s,
    v_s,
    normed_s,
    q_s,
    key_s,
    value_s,
    attn_s,
    low_send,
    low_recv,
    share_send,
    share_recv,
    in_sem,
    w_sem,
    kv_sem,
    wo_sem,
    own_sem,
    gather_send,
    gather_recv,
    relay_send,
    relay_recv,
    low_send_sem,
    low_recv_sem,
    share_send_sem,
    share_recv_sem,
):
    d = lax.axis_index("dp")
    t = lax.axis_index("tp")
    rows, features = x_hbm.shape
    rank = qd_hbm.shape[0]
    groups = k_hbm.shape[1]
    cache = k_hbm.shape[2]
    width = wq_hbm.shape[1]
    heads = width // HEAD_SIZE
    per_group = heads // groups
    pieces = w_sem.shape[1]
    depth = features // pieces
    columns = base_ref.shape[1]
    f32, bf16 = jnp.float32, jnp.bfloat16

    small = [
        pltpu.make_async_copy(src, dst, in_sem.at[i])
        for i, (src, dst) in enumerate(((x_hbm, x_s), (gain_hbm, gain_s), (lengths_hbm, lengths_s)))
    ]
    for copy in small:
        copy.start()

    def weight_copies(k):
        span = pl.ds(pl.multiple_of(k * depth, depth), depth)
        return [
            pltpu.make_async_copy(src.at[span], dst.at[span], w_sem.at[i, k])
            for i, (src, dst) in enumerate(((wq_hbm, wq_s), (wk_hbm, wk_s), (wv_hbm, wv_s)))
        ]

    def cache_copies(r):
        return [
            pltpu.make_async_copy(src.at[r], dst.at[r], kv_sem.at[i, r])
            for i, (src, dst) in enumerate(((k_hbm, k_s), (v_hbm, v_s)))
        ]

    halves = wo_sem.shape[1]
    half_rows = width // halves

    def out_copy(step, half):
        to = lax.rem(t + 1 + step, tp)
        span = pl.ds(pl.multiple_of(half * half_rows, half_rows), half_rows)
        return pltpu.make_async_copy(
            wo_hbm.at[span, pl.ds(pl.multiple_of(to * columns, columns), columns)],
            wo_s.at[step, span],
            wo_sem.at[step, half],
        )

    ahead = pieces // 2
    for k in range(ahead):
        for copy in weight_copies(k):
            copy.start()

    factors = ((qd_hbm, qd_s), (qu_hbm, qu_s), (od_hbm, od_s), (ou_hbm, ou_s))
    own = [
        pltpu.make_async_copy(src, dst.at[d], own_sem.at[i]) for i, (src, dst) in enumerate(factors)
    ]
    for copy in own:
        copy.start()

    chips = dp // 2
    sibling = d + 1 - 2 * lax.rem(d, 2)

    def same_core(i):
        return lax.rem(d + 2 * i, dp)

    barrier = pltpu.get_barrier_semaphore()
    peers = [(same_core(i), t) for i in range(1, chips)] + [(sibling, t)]
    peers += [(d, lax.rem(t + i, tp)) for i in range(1, tp)]
    for peer in peers:
        pl.semaphore_signal(
            barrier, inc=1, device_id=peer, device_id_type=pl.DeviceIdType.MESH
        )

    for copy in small:
        copy.wait()
    hidden = x_s[...].astype(f32)
    normed_s[...] = (
        hidden
        * lax.rsqrt(jnp.mean(hidden * hidden, axis=-1, keepdims=True) + 1e-05)
        * gain_s[...]
    ).astype(bf16)

    lengths = jnp.sum(
        jnp.where(
            lax.broadcasted_iota(jnp.int32, (rows, rows), 0)
            == lax.broadcasted_iota(jnp.int32, (rows, rows), 1),
            jnp.broadcast_to(lengths_s[...].astype(f32), (rows, rows)),
            0.0,
        ),
        axis=1,
        keepdims=True,
    )
    lane = lax.broadcasted_iota(jnp.int32, (rows, HEAD_SIZE), 1)
    first = lane < HEAD_SIZE // 2
    number = jnp.where(first, lane, lane - HEAD_SIZE // 2).astype(f32)
    angles = lengths * jnp.exp(number * (-2.0 * math.log(rope_theta) / HEAD_SIZE))
    table_s[:, :HEAD_SIZE] = jnp.cos(angles)
    table_s[:, HEAD_SIZE:] = jnp.where(first, -jnp.sin(angles), jnp.sin(angles))
    key_s[:, groups, :] = jnp.broadcast_to(lengths, (rows, HEAD_SIZE))

    pl.semaphore_wait(barrier, len(peers))

    def gather(which, i):
        src, dst = factors[which]
        return pltpu.make_async_remote_copy(
            src_ref=src,
            dst_ref=dst.at[d],
            send_sem=gather_send.at[which, i],
            recv_sem=gather_recv.at[which, i],
            device_id=(same_core(i), t),
            device_id_type=pl.DeviceIdType.MESH,
        )

    def relayed(which, i, core):
        dst = factors[which][1]
        slot = lax.rem(core + dp - 2 * i, dp)
        return pltpu.make_async_remote_copy(
            src_ref=dst.at[slot] if i else factors[which][0],
            dst_ref=dst.at[slot],
            send_sem=relay_send.at[which, i],
            recv_sem=relay_recv.at[which, i],
            device_id=(sibling, t),
            device_id_type=pl.DeviceIdType.MESH,
        )

    def arrived(which, i):
        src, dst = factors[which]
        return pltpu.make_async_remote_copy(
            src_ref=src,
            dst_ref=dst.at[lax.rem(d + dp - 2 * i, dp)],
            send_sem=gather_send.at[which, i],
            recv_sem=gather_recv.at[which, i],
            device_id=(same_core(i), t),
            device_id_type=pl.DeviceIdType.MESH,
        )

    def spread(which):
        for i in range(1, chips):
            gather(which, i).start()
        relayed(which, 0, d).start()

    def relay(which):
        for i in range(1, chips):
            arrived(which, i).wait_recv()
            relayed(which, i, d).start()

    def take(which):
        own[which].wait()
        for i in range(chips):
            relayed(which, i, sibling).wait_recv()

    spread(0)
    spread(1)

    def project(k, totals):
        for copy in weight_copies(k):
            copy.wait()

        @pl.when(k < pieces - ahead)
        def _():
            for copy in weight_copies(k + ahead):
                copy.start()

        @pl.when(k >= pieces - ahead)
        def _():
            for u in range(2):
                for copy in cache_copies((k - (pieces - ahead)) * 2 + u):
                    copy.start()

        span = pl.ds(pl.multiple_of(k * depth, depth), depth)
        block = normed_s[:, span]
        return tuple(
            total + jnp.dot(block, weight[span, :], preferred_element_type=f32)
            for total, weight in zip(totals, (wq_s, wk_s, wv_s))
        )

    totals = tuple(jnp.zeros((rows, w.shape[1]), f32) for w in (wq_s, wk_s, wv_s))
    totals = lax.fori_loop(0, pieces // 2, project, totals)

    relay(0)
    relay(1)
    take(0)
    part_width = qd_hbm.shape[1]
    part = jnp.zeros((rows, rank), f32)
    for i in range(dp):
        at = pl.multiple_of((i * tp + t) * part_width, part_width)
        part += lax.dot_general(
            normed_s[:, pl.ds(at, part_width)],
            qd_s[i],
            (((1,), (1,)), ((), ())),
            preferred_element_type=f32,
        )
    low_send[...] = jnp.concatenate(
        [part, jnp.zeros((rows, HEAD_SIZE - rank), f32)], axis=1
    )

    def low_copy(step):
        return pltpu.make_async_remote_copy(
            src_ref=low_send,
            dst_ref=low_recv.at[step],
            send_sem=low_send_sem.at[step],
            recv_sem=low_recv_sem.at[step],
            device_id=(d, lax.rem(t + 1 + step, tp)),
            device_id_type=pl.DeviceIdType.MESH,
        )

    for step in range(tp - 1):
        low_copy(step).start()

    totals = lax.fori_loop(pieces // 2, pieces, project, totals)
    query_total, key_total, value_total = totals
    cosine = table_s[:, :HEAD_SIZE]
    sine = table_s[:, HEAD_SIZE:]

    def turned(vectors):
        rolled = pltpu.roll(vectors, HEAD_SIZE // 2, 1)
        return (vectors * cosine + rolled * sine).astype(bf16).astype(f32)

    for g in range(groups):
        span = slice(g * HEAD_SIZE, (g + 1) * HEAD_SIZE)
        key_s[:, g, :] = turned(key_total[:, span])
        value_s[:, g, :] = value_total[:, span].astype(bf16).astype(f32)

    spread(2)
    spread(3)
    take(1)
    low = low_send[...]
    for step in range(tp - 1):
        low_copy(step).wait_recv()
        low += low_recv[step]
    parts = three_parts(low[:, :rank])
    up_width = qu_hbm.shape[1]
    for i in range(dp):
        extra = wide_product(parts, qu_s[i], rows)
        for j in range(up_width // HEAD_SIZE):
            h = i * (up_width // HEAD_SIZE) + j
            base = query_total[:, h * HEAD_SIZE : (h + 1) * HEAD_SIZE]
            q_s[:, h, :] = turned(
                base + adapter_scale * extra[:, j * HEAD_SIZE : (j + 1) * HEAD_SIZE]
            )

    scale = HEAD_SIZE ** (-0.5)
    at_once = 4
    units_each = tp * halves * at_once // rows

    def attend(step, carry):
        for u in range(at_once):
            for copy in cache_copies(step * at_once + u):
                copy.wait()
        for u in range(units_each):
            unit = step * units_each + u
            out_copy(unit // halves, unit % halves).start()
        pairs = [(step * at_once + u, g) for u in range(at_once) for g in range(groups)]
        count = len(pairs) * per_group

        def stacked(blocks):
            return jnp.concatenate(blocks, axis=0)

        def spread_out(ref, place):
            return stacked(
                [
                    jnp.broadcast_to(
                        ref[r, pl.ds(g if place is None else place, 1), :],
                        (per_group, HEAD_SIZE),
                    )
                    for r, g in pairs
                ]
            )

        queries = [q_s[r, g * per_group : (g + 1) * per_group, :] for r, g in pairs]
        scores = stacked(
            [
                lax.dot_general(
                    query.astype(bf16),
                    k_s[r, g],
                    (((1,), (1,)), ((), ())),
                    preferred_element_type=f32,
                )
                for query, (r, g) in zip(queries, pairs)
            ]
        )
        mine = (
            jnp.sum(stacked(queries) * spread_out(key_s, None), axis=-1, keepdims=True) * scale
        )
        reach = spread_out(key_s, groups)[:, :1]
        seat = lax.broadcasted_iota(jnp.int32, (count, cache), 1).astype(f32)
        scores = jnp.where(seat < reach, scores * scale, -jnp.inf)
        top = jnp.maximum(jnp.max(scores, axis=-1, keepdims=True), mine)
        powers = jnp.exp(scores - top)
        my_power = jnp.exp(mine - top)
        inverse = 1.0 / (jnp.sum(powers, axis=-1, keepdims=True) + my_power)
        weights = powers * inverse
        my_weight = (my_power * inverse).astype(bf16).astype(f32)
        mixed = stacked(
            [
                jnp.dot(
                    weights[n * per_group : (n + 1) * per_group].astype(bf16),
                    v_s[r, g],
                    preferred_element_type=f32,
                )
                for n, (r, g) in enumerate(pairs)
            ]
        )
        mixed = mixed + my_weight * spread_out(value_s, None)
        mixed = mixed.astype(bf16).astype(f32)
        for n, (r, g) in enumerate(pairs):
            attn_s[g * per_group : (g + 1) * per_group, r, :] = mixed[
                n * per_group : (n + 1) * per_group
            ]
        return carry

    lax.fori_loop(0, rows // at_once // 2, attend, 0)
    relay(2)
    relay(3)
    lax.fori_loop(rows // at_once // 2, rows // at_once, attend, 0)

    flat = jnp.concatenate([attn_s[h] for h in range(heads)], axis=1).astype(bf16)

    take(2)
    down_rows = od_hbm.shape[1]
    low_o = jnp.zeros((rows, rank), f32)
    for i in range(dp):
        low_o += lax.dot_general(
            flat[:, i * down_rows : (i + 1) * down_rows],
            od_s[i],
            (((1,), (1,)), ((), ())),
            preferred_element_type=f32,
        )
    low_o = jnp.concatenate([low_o, jnp.zeros((rows, HEAD_SIZE - rank), f32)], axis=1)

    def share_copy(step):
        return pltpu.make_async_remote_copy(
            src_ref=share_send.at[step],
            dst_ref=share_recv.at[step],
            send_sem=share_send_sem.at[step],
            recv_sem=share_recv_sem.at[step],
            device_id=(d, lax.rem(t + 1 + step, tp)),
            device_id_type=pl.DeviceIdType.MESH,
        )

    tile = 256
    for step in range(tp):
        for half in range(halves):
            out_copy(step, half).wait()

        def columns_of(c, carry, step=step):
            span = pl.ds(pl.multiple_of(c * tile, tile), tile)
            share_send[step, :, span] = jnp.dot(
                flat, wo_s[step, :, span], preferred_element_type=f32
            )
            return carry

        lax.fori_loop(0, columns // tile, columns_of, 0)
        share_send[step, :, columns:] = low_o
        if step < tp - 1:
            share_copy(step).start()

    take(3)
    total = share_send[tp - 1]
    for step in range(tp - 1):
        share_copy(step).wait_recv()
        total += share_recv[step]
    parts = three_parts(total[:, columns : columns + rank])
    last_width = ou_hbm.shape[1]
    for i in range(dp):
        span = slice(i * last_width, (i + 1) * last_width)
        extra_ref[:, span] = adapter_scale * wide_product(parts, ou_s[i], rows)
    base_ref[...] = total[:, :columns]

    for which in range(len(factors)):
        for i in range(1, chips):
            gather(which, i).wait_send()
        for i in range(chips):
            relayed(which, i, d).wait_send()
    for step in range(tp - 1):
        low_copy(step).wait_send()
        share_copy(step).wait_send()


def on_device(
    residual_hidden,
    attention_norm_gain,
    query_matrix,
    key_matrix,
    value_matrix,
    output_matrix,
    query_adapter_down,
    query_adapter_up,
    output_adapter_down,
    output_adapter_up,
    cached_rotated_keys,
    cached_value_rows,
    cache_fill_lengths,
):
    dp, tp = lax.axis_size("dp"), lax.axis_size("tp")
    rows, features = residual_hidden.shape
    width = query_matrix.shape[1]
    heads = width // HEAD_SIZE
    groups = key_matrix.shape[1] // HEAD_SIZE
    columns = output_matrix.shape[1] // tp
    pieces = rows
    bf16, f32 = jnp.bfloat16, jnp.float32
    operands = (
        residual_hidden,
        attention_norm_gain.reshape(1, features),
        cache_fill_lengths.reshape(1, rows),
        query_matrix,
        key_matrix,
        value_matrix,
        output_matrix,
        query_adapter_down.T,
        query_adapter_up,
        output_adapter_down.T,
        output_adapter_up,
        cached_rotated_keys,
        cached_value_rows,
    )
    base, extra = pl.pallas_call(
        functools.partial(kernel, dp, tp),
        out_shape=[pltpu.VMEM((rows, columns), f32)] * 2,
        in_specs=[pl.BlockSpec(memory_space=pl.ANY)] * len(operands),
        out_specs=[pl.BlockSpec(memory_space=pltpu.VMEM)] * 2,
        scratch_shapes=[
            pltpu.VMEM(residual_hidden.shape, bf16),
            pltpu.VMEM((1, features), f32),
            pltpu.VMEM((1, rows), jnp.int32),
            pltpu.VMEM((rows, 2 * HEAD_SIZE), f32),
            pltpu.VMEM(query_matrix.shape, bf16),
            pltpu.VMEM(key_matrix.shape, bf16),
            pltpu.VMEM(value_matrix.shape, bf16),
            pltpu.VMEM((tp, width, columns), bf16),
            pltpu.VMEM((dp,) + query_adapter_down.shape[::-1], bf16),
            pltpu.VMEM((dp,) + query_adapter_up.shape, bf16),
            pltpu.VMEM((dp,) + output_adapter_down.shape[::-1], bf16),
            pltpu.VMEM((dp,) + output_adapter_up.shape, bf16),
            pltpu.VMEM(cached_rotated_keys.shape, bf16),
            pltpu.VMEM(cached_value_rows.shape, bf16),
            pltpu.VMEM((rows, features), bf16),
            pltpu.VMEM((rows, heads, HEAD_SIZE), f32),
            pltpu.VMEM((rows, groups + 1, HEAD_SIZE), f32),
            pltpu.VMEM((rows, groups, HEAD_SIZE), f32),
            pltpu.VMEM((heads, rows, HEAD_SIZE), f32),
            pltpu.VMEM((rows, HEAD_SIZE), f32),
            pltpu.VMEM((tp - 1, rows, HEAD_SIZE), f32),
            pltpu.VMEM((tp, rows, columns + HEAD_SIZE), f32),
            pltpu.VMEM((tp - 1, rows, columns + HEAD_SIZE), f32),
            pltpu.SemaphoreType.DMA((3,)),
            pltpu.SemaphoreType.DMA((3, pieces)),
            pltpu.SemaphoreType.DMA((2, rows)),
            pltpu.SemaphoreType.DMA((tp, 2)),
            pltpu.SemaphoreType.DMA((4,)),
            pltpu.SemaphoreType.DMA((4, dp // 2)),
            pltpu.SemaphoreType.DMA((4, dp // 2)),
            pltpu.SemaphoreType.DMA((4, dp // 2)),
            pltpu.SemaphoreType.DMA((4, dp // 2)),
            pltpu.SemaphoreType.DMA((tp - 1,)),
            pltpu.SemaphoreType.DMA((tp - 1,)),
            pltpu.SemaphoreType.DMA((tp - 1,)),
            pltpu.SemaphoreType.DMA((tp - 1,)),
        ],
        compiler_params=pltpu.CompilerParams(
            collective_id=0, has_side_effects=True, vmem_limit_bytes=56 * 1024 * 1024
        ),
    )(*operands)
    return base + extra


def solution(mesh):
    in_specs = (
        P("dp", None),
        P(),
        P(None, "tp"),
        P(None, "tp"),
        P(None, "tp"),
        P("tp", None),
        P(("dp", "tp"), None),
        P(None, ("tp", "dp")),
        P(("tp", "dp"), None),
        P(None, ("tp", "dp")),
        P("dp", "tp", None, None),
        P("dp", "tp", None, None),
        P("dp"),
    )
    out_specs = P("dp", "tp")

    def local(*arrays):
        wide = arrays[7].shape[1] % HEAD_SIZE == 0 and arrays[9].shape[1] % HEAD_SIZE == 0
        return (on_device if wide else on_device_narrow)(*arrays)

    return jax.shard_map(
        local, mesh=mesh, in_specs=in_specs, out_specs=out_specs, check_vma=False
    )
```

```python
import functools
import math

import jax
import jax.numpy as jnp
from jax import lax
from jax.experimental import pallas as pl
from jax.experimental.pallas import tpu as pltpu
from jax.sharding import PartitionSpec as P

HEAD_SIZE = 128


adapter_scale = 2.0
rope_theta = 500000.0


def rotate(vectors, positions):
    half_dim = vectors.shape[-1] // 2
    steps_idx = jnp.arange(half_dim, dtype=jnp.float32)
    inverse = jnp.exp(steps_idx * (-2.0 * math.log(rope_theta) / vectors.shape[-1]))
    angles = positions[:, None, None] * inverse[None, None, :]
    cosine = jnp.cos(angles)
    sine = jnp.sin(angles)
    first = vectors[..., :half_dim]
    second = vectors[..., half_dim:]
    return jnp.concatenate(
        [first * cosine - second * sine, second * cosine + first * sine], axis=-1
    )


def on_device_narrow(
    residual_hidden,
    attention_norm_gain,
    query_matrix,
    key_matrix,
    value_matrix,
    output_matrix,
    query_adapter_down,
    query_adapter_up,
    output_adapter_down,
    output_adapter_up,
    cached_rotated_keys,
    cached_value_rows,
    cache_fill_lengths,
):
    row_count = residual_hidden.shape[0]
    feature_width = residual_hidden.shape[1]
    rank_width = query_adapter_down.shape[1]
    local_heads = query_matrix.shape[1] // HEAD_SIZE
    local_groups = key_matrix.shape[1] // HEAD_SIZE
    group_size = local_heads // local_groups
    cache_length = cached_rotated_keys.shape[2]
    hidden_f = residual_hidden.astype(jnp.float32)
    normalized_hidden = (
        hidden_f
        * lax.rsqrt(jnp.mean(hidden_f * hidden_f, axis=-1, keepdims=True) + 1e-05)
        * attention_norm_gain
    ).astype(jnp.bfloat16)
    q_up_local, o_down_local = (
        lax.all_gather(query_adapter_up, "dp", axis=1, tiled=True),
        lax.all_gather(output_adapter_down, "dp", axis=0, tiled=True),
    )
    q_down_share = lax.all_gather(query_adapter_down, "dp", axis=0, tiled=True)
    dp_count = lax.axis_size("dp")
    tp_count = lax.axis_size("tp")
    block_width = feature_width // (dp_count * tp_count)
    picked = lax.dynamic_index_in_dim(
        normalized_hidden.reshape(row_count, dp_count, tp_count, block_width),
        lax.axis_index("tp"),
        2,
        keepdims=False,
    )
    partial_low = jnp.einsum(
        "rdb,dbk->rk",
        picked,
        q_down_share.reshape(dp_count, block_width, rank_width),
        preferred_element_type=jnp.float32,
    )
    query_low_rank = lax.psum(partial_low, "tp")
    query_rows = jnp.dot(
        normalized_hidden, query_matrix, preferred_element_type=jnp.float32
    ) + adapter_scale * jnp.dot(
        query_low_rank, q_up_local.astype(jnp.float32), precision=lax.Precision.HIGHEST
    )
    keys_new = jnp.dot(normalized_hidden, key_matrix, preferred_element_type=jnp.float32)
    values_new = jnp.dot(
        normalized_hidden, value_matrix, preferred_element_type=jnp.float32
    ).astype(jnp.bfloat16)
    positions = cache_fill_lengths.astype(jnp.float32)
    query_rot = (
        rotate(query_rows.reshape(row_count, local_heads, HEAD_SIZE), positions)
        .astype(jnp.bfloat16)
        .reshape(row_count, local_groups, group_size, HEAD_SIZE)
    )
    key_rot = rotate(keys_new.reshape(row_count, local_groups, HEAD_SIZE), positions).astype(
        jnp.bfloat16
    )
    value_rows = values_new.reshape(row_count, local_groups, HEAD_SIZE)
    score_scale = HEAD_SIZE ** (-0.5)
    scores = (
        jnp.einsum(
            "rkgd,rkcd->rkgc", query_rot, cached_rotated_keys, preferred_element_type=jnp.float32
        )
        * score_scale
    )
    visible = (
        jnp.arange(cache_length, dtype=jnp.int32)[None, None, None, :]
        < cache_fill_lengths[:, None, None, None]
    )
    scores = jnp.where(visible, scores, -jnp.inf)
    own_score = (
        jnp.einsum("rkgd,rkd->rkg", query_rot, key_rot, preferred_element_type=jnp.float32)
        * score_scale
    )
    top_score = jnp.maximum(jnp.max(scores, axis=-1), own_score)
    cache_exp = jnp.exp(scores - top_score[..., None])
    own_exp = jnp.exp(own_score - top_score)
    denominator = jnp.sum(cache_exp, axis=-1) + own_exp
    cache_weight = (cache_exp / denominator[..., None]).astype(jnp.bfloat16)
    own_weight = (own_exp / denominator).astype(jnp.bfloat16)
    attn = jnp.einsum(
        "rkgc,rkcd->rkgd", cache_weight, cached_value_rows, preferred_element_type=jnp.float32
    )
    attn = (
        attn
        + own_weight.astype(jnp.float32)[..., None] * value_rows.astype(jnp.float32)[:, :, None, :]
    )
    attention_flattened = attn.astype(jnp.bfloat16).reshape(row_count, local_heads * HEAD_SIZE)
    low_o_part = jnp.dot(attention_flattened, o_down_local, preferred_element_type=jnp.float32)
    base_contribution = jnp.dot(
        attention_flattened, output_matrix, preferred_element_type=jnp.float32
    )
    output_low_rank = lax.psum(low_o_part, "tp")
    o_up_own = lax.all_gather(output_adapter_up, "dp", axis=1, tiled=True)
    attn_out = lax.psum_scatter(
        base_contribution, "tp", scatter_dimension=1, tiled=True
    ) + adapter_scale * jnp.dot(
        output_low_rank, o_up_own.astype(jnp.float32), precision=lax.Precision.HIGHEST
    )
    return attn_out


def three_parts(values):
    high = values.astype(jnp.bfloat16)
    rest = values - high.astype(jnp.float32)
    middle = rest.astype(jnp.bfloat16)
    low = (rest - middle.astype(jnp.float32)).astype(jnp.bfloat16)
    return jnp.concatenate(
        [high.astype(jnp.float32), middle.astype(jnp.float32), low.astype(jnp.float32)], axis=0
    ).astype(jnp.bfloat16)


def wide_product(parts, right, rows):
    product = jnp.dot(parts, right, preferred_element_type=jnp.float32)
    return product[:rows] + (product[rows : 2 * rows] + product[2 * rows :])


def kernel(
    dp,
    tp,
    x_hbm,
    gain_hbm,
    lengths_hbm,
    wq_hbm,
    wk_hbm,
    wv_hbm,
    wo_hbm,
    qd_hbm,
    qu_hbm,
    od_hbm,
    ou_hbm,
    k_hbm,
    v_hbm,
    base_ref,
    extra_ref,
    x_s,
    gain_s,
    lengths_s,
    table_s,
    wq_s,
    wk_s,
    wv_s,
    wo_s,
    qd_s,
    qu_s,
    od_s,
    ou_s,
    k_s,
    v_s,
    normed_s,
    q_s,
    key_s,
    value_s,
    attn_s,
    low_send,
    low_recv,
    share_send,
    share_recv,
    in_sem,
    w_sem,
    kv_sem,
    wo_sem,
    own_sem,
    gather_send,
    gather_recv,
    relay_send,
    relay_recv,
    low_send_sem,
    low_recv_sem,
    share_send_sem,
    share_recv_sem,
):
    d = lax.axis_index("dp")
    t = lax.axis_index("tp")
    rows, features = x_hbm.shape
    rank = qd_hbm.shape[0]
    groups = k_hbm.shape[1]
    cache = k_hbm.shape[2]
    width = wq_hbm.shape[1]
    heads = width // HEAD_SIZE
    per_group = heads // groups
    pieces = w_sem.shape[1]
    depth = features // pieces
    columns = base_ref.shape[1]
    f32, bf16 = jnp.float32, jnp.bfloat16

    small = [
        pltpu.make_async_copy(src, dst, in_sem.at[i])
        for i, (src, dst) in enumerate(((x_hbm, x_s), (gain_hbm, gain_s), (lengths_hbm, lengths_s)))
    ]
    for copy in small:
        copy.start()

    def weight_copies(k):
        span = pl.ds(pl.multiple_of(k * depth, depth), depth)
        return [
            pltpu.make_async_copy(src.at[span], dst.at[span], w_sem.at[i, k])
            for i, (src, dst) in enumerate(((wq_hbm, wq_s), (wk_hbm, wk_s), (wv_hbm, wv_s)))
        ]

    def cache_copies(r):
        return [
            pltpu.make_async_copy(src.at[r], dst.at[r], kv_sem.at[i, r])
            for i, (src, dst) in enumerate(((k_hbm, k_s), (v_hbm, v_s)))
        ]

    halves = wo_sem.shape[1]
    half_rows = width // halves

    def out_copy(step, half):
        to = lax.rem(t + 1 + step, tp)
        span = pl.ds(pl.multiple_of(half * half_rows, half_rows), half_rows)
        return pltpu.make_async_copy(
            wo_hbm.at[span, pl.ds(pl.multiple_of(to * columns, columns), columns)],
            wo_s.at[step, span],
            wo_sem.at[step, half],
        )

    ahead = pieces // 2
    for k in range(ahead):
        for copy in weight_copies(k):
            copy.start()

    factors = ((qd_hbm, qd_s), (qu_hbm, qu_s), (od_hbm, od_s), (ou_hbm, ou_s))
    own = [
        pltpu.make_async_copy(src, dst.at[d], own_sem.at[i]) for i, (src, dst) in enumerate(factors)
    ]
    for copy in own:
        copy.start()

    chips = dp // 2
    sibling = d + 1 - 2 * lax.rem(d, 2)

    def same_core(i):
        return lax.rem(d + 2 * i, dp)

    barrier = pltpu.get_barrier_semaphore()
    peers = [(same_core(i), t) for i in range(1, chips)] + [(sibling, t)]
    peers += [(d, lax.rem(t + i, tp)) for i in range(1, tp)]
    for peer in peers:
        pl.semaphore_signal(
            barrier, inc=1, device_id=peer, device_id_type=pl.DeviceIdType.MESH
        )

    for copy in small:
        copy.wait()
    hidden = x_s[...].astype(f32)
    normed_s[...] = (
        hidden
        * lax.rsqrt(jnp.mean(hidden * hidden, axis=-1, keepdims=True) + 1e-05)
        * gain_s[...]
    ).astype(bf16)

    lengths = jnp.sum(
        jnp.where(
            lax.broadcasted_iota(jnp.int32, (rows, rows), 0)
            == lax.broadcasted_iota(jnp.int32, (rows, rows), 1),
            jnp.broadcast_to(lengths_s[...].astype(f32), (rows, rows)),
            0.0,
        ),
        axis=1,
        keepdims=True,
    )
    lane = lax.broadcasted_iota(jnp.int32, (rows, HEAD_SIZE), 1)
    first = lane < HEAD_SIZE // 2
    number = jnp.where(first, lane, lane - HEAD_SIZE // 2).astype(f32)
    angles = lengths * jnp.exp(number * (-2.0 * math.log(rope_theta) / HEAD_SIZE))
    table_s[:, :HEAD_SIZE] = jnp.cos(angles)
    table_s[:, HEAD_SIZE:] = jnp.where(first, -jnp.sin(angles), jnp.sin(angles))
    key_s[:, groups, :] = jnp.broadcast_to(lengths, (rows, HEAD_SIZE))

    pl.semaphore_wait(barrier, len(peers))

    def gather(which, i):
        src, dst = factors[which]
        return pltpu.make_async_remote_copy(
            src_ref=src,
            dst_ref=dst.at[d],
            send_sem=gather_send.at[which, i],
            recv_sem=gather_recv.at[which, i],
            device_id=(same_core(i), t),
            device_id_type=pl.DeviceIdType.MESH,
        )

    def relayed(which, i, core):
        dst = factors[which][1]
        slot = lax.rem(core + dp - 2 * i, dp)
        return pltpu.make_async_remote_copy(
            src_ref=dst.at[slot] if i else factors[which][0],
            dst_ref=dst.at[slot],
            send_sem=relay_send.at[which, i],
            recv_sem=relay_recv.at[which, i],
            device_id=(sibling, t),
            device_id_type=pl.DeviceIdType.MESH,
        )

    def arrived(which, i):
        src, dst = factors[which]
        return pltpu.make_async_remote_copy(
            src_ref=src,
            dst_ref=dst.at[lax.rem(d + dp - 2 * i, dp)],
            send_sem=gather_send.at[which, i],
            recv_sem=gather_recv.at[which, i],
            device_id=(same_core(i), t),
            device_id_type=pl.DeviceIdType.MESH,
        )

    def spread(which):
        for i in range(1, chips):
            gather(which, i).start()
        relayed(which, 0, d).start()

    def relay(which):
        for i in range(1, chips):
            arrived(which, i).wait_recv()
            relayed(which, i, d).start()

    def take(which):
        own[which].wait()
        for i in range(chips):
            relayed(which, i, sibling).wait_recv()

    spread(0)
    spread(1)

    def project(k, totals):
        for copy in weight_copies(k):
            copy.wait()

        @pl.when(k < pieces - ahead)
        def _():
            for copy in weight_copies(k + ahead):
                copy.start()

        @pl.when(k >= pieces - ahead)
        def _():
            for u in range(2):
                for copy in cache_copies((k - (pieces - ahead)) * 2 + u):
                    copy.start()

        span = pl.ds(pl.multiple_of(k * depth, depth), depth)
        block = normed_s[:, span]
        return tuple(
            total + jnp.dot(block, weight[span, :], preferred_element_type=f32)
            for total, weight in zip(totals, (wq_s, wk_s, wv_s))
        )

    totals = tuple(jnp.zeros((rows, w.shape[1]), f32) for w in (wq_s, wk_s, wv_s))
    totals = lax.fori_loop(0, pieces // 2, project, totals)

    relay(0)
    take(0)
    part_width = qd_hbm.shape[1]
    part = jnp.zeros((rows, rank), f32)
    for i in range(dp):
        at = pl.multiple_of((i * tp + t) * part_width, part_width)
        part += lax.dot_general(
            normed_s[:, pl.ds(at, part_width)],
            qd_s[i],
            (((1,), (1,)), ((), ())),
            preferred_element_type=f32,
        )
    low_send[...] = jnp.concatenate(
        [part, jnp.zeros((rows, HEAD_SIZE - rank), f32)], axis=1
    )

    def low_copy(step):
        return pltpu.make_async_remote_copy(
            src_ref=low_send,
            dst_ref=low_recv.at[step],
            send_sem=low_send_sem.at[step],
            recv_sem=low_recv_sem.at[step],
            device_id=(d, lax.rem(t + 1 + step, tp)),
            device_id_type=pl.DeviceIdType.MESH,
        )

    for step in range(tp - 1):
        low_copy(step).start()
    relay(1)
    spread(2)
    spread(3)

    totals = lax.fori_loop(pieces // 2, pieces, project, totals)
    query_total, key_total, value_total = totals
    cosine = table_s[:, :HEAD_SIZE]
    sine = table_s[:, HEAD_SIZE:]

    def turned(vectors):
        rolled = pltpu.roll(vectors, HEAD_SIZE // 2, 1)
        return (vectors * cosine + rolled * sine).astype(bf16).astype(f32)

    for g in range(groups):
        span = slice(g * HEAD_SIZE, (g + 1) * HEAD_SIZE)
        key_s[:, g, :] = turned(key_total[:, span])
        value_s[:, g, :] = value_total[:, span].astype(bf16).astype(f32)

    take(1)
    for unit in range(tp * halves):
        out_copy(unit // halves, unit % halves).start()
    low = low_send[...]
    for step in range(tp - 1):
        low_copy(step).wait_recv()
        low += low_recv[step]
    parts = three_parts(low[:, :rank])
    up_width = qu_hbm.shape[1]
    for i in range(dp):
        extra = wide_product(parts, qu_s[i], rows)
        for j in range(up_width // HEAD_SIZE):
            h = i * (up_width // HEAD_SIZE) + j
            base = query_total[:, h * HEAD_SIZE : (h + 1) * HEAD_SIZE]
            q_s[:, h, :] = turned(
                base + adapter_scale * extra[:, j * HEAD_SIZE : (j + 1) * HEAD_SIZE]
            )

    scale = HEAD_SIZE ** (-0.5)
    at_once = 4

    def attend(step, carry):
        for u in range(at_once):
            for copy in cache_copies(step * at_once + u):
                copy.wait()
        pairs = [(step * at_once + u, g) for u in range(at_once) for g in range(groups)]
        count = len(pairs) * per_group

        def stacked(blocks):
            return jnp.concatenate(blocks, axis=0)

        def spread_out(ref, place):
            return stacked(
                [
                    jnp.broadcast_to(
                        ref[r, pl.ds(g if place is None else place, 1), :],
                        (per_group, HEAD_SIZE),
                    )
                    for r, g in pairs
                ]
            )

        queries = [q_s[r, g * per_group : (g + 1) * per_group, :] for r, g in pairs]
        scores = stacked(
            [
                lax.dot_general(
                    query.astype(bf16),
                    k_s[r, g],
                    (((1,), (1,)), ((), ())),
                    preferred_element_type=f32,
                )
                for query, (r, g) in zip(queries, pairs)
            ]
        )
        mine = (
            jnp.sum(stacked(queries) * spread_out(key_s, None), axis=-1, keepdims=True) * scale
        )
        reach = spread_out(key_s, groups)[:, :1]
        seat = lax.broadcasted_iota(jnp.int32, (count, cache), 1).astype(f32)
        scores = jnp.where(seat < reach, scores * scale, -jnp.inf)
        top = jnp.maximum(jnp.max(scores, axis=-1, keepdims=True), mine)
        powers = jnp.exp(scores - top)
        my_power = jnp.exp(mine - top)
        inverse = 1.0 / (jnp.sum(powers, axis=-1, keepdims=True) + my_power)
        weights = powers * inverse
        my_weight = (my_power * inverse).astype(bf16).astype(f32)
        mixed = stacked(
            [
                jnp.dot(
                    weights[n * per_group : (n + 1) * per_group].astype(bf16),
                    v_s[r, g],
                    preferred_element_type=f32,
                )
                for n, (r, g) in enumerate(pairs)
            ]
        )
        mixed = mixed + my_weight * spread_out(value_s, None)
        mixed = mixed.astype(bf16).astype(f32)
        for n, (r, g) in enumerate(pairs):
            attn_s[g * per_group : (g + 1) * per_group, r, :] = mixed[
                n * per_group : (n + 1) * per_group
            ]
        return carry

    lax.fori_loop(0, rows // at_once // 2, attend, 0)
    relay(2)
    relay(3)
    lax.fori_loop(rows // at_once // 2, rows // at_once, attend, 0)

    flat = jnp.concatenate([attn_s[h] for h in range(heads)], axis=1).astype(bf16)

    take(2)
    down_rows = od_hbm.shape[1]
    low_o = jnp.zeros((rows, rank), f32)
    for i in range(dp):
        low_o += lax.dot_general(
            flat[:, i * down_rows : (i + 1) * down_rows],
            od_s[i],
            (((1,), (1,)), ((), ())),
            preferred_element_type=f32,
        )
    low_o = jnp.concatenate([low_o, jnp.zeros((rows, HEAD_SIZE - rank), f32)], axis=1)

    def share_copy(step):
        return pltpu.make_async_remote_copy(
            src_ref=share_send.at[step],
            dst_ref=share_recv.at[step],
            send_sem=share_send_sem.at[step],
            recv_sem=share_recv_sem.at[step],
            device_id=(d, lax.rem(t + 1 + step, tp)),
            device_id_type=pl.DeviceIdType.MESH,
        )

    tile = 512
    for step in range(tp):
        for half in range(halves):
            out_copy(step, half).wait()

        def columns_of(c, carry, step=step):
            span = pl.ds(pl.multiple_of(c * tile, tile), tile)
            share_send[step, :, span] = jnp.dot(
                flat, wo_s[step, :, span], preferred_element_type=f32
            )
            return carry

        lax.fori_loop(0, columns // tile, columns_of, 0)
        share_send[step, :, columns:] = low_o
        if step < tp - 1:
            share_copy(step).start()

    take(3)
    total = share_send[tp - 1]
    for step in range(tp - 1):
        share_copy(step).wait_recv()
        total += share_recv[step]
    parts = three_parts(total[:, columns : columns + rank])
    last_width = ou_hbm.shape[1]
    for i in range(dp):
        span = slice(i * last_width, (i + 1) * last_width)
        extra_ref[:, span] = adapter_scale * wide_product(parts, ou_s[i], rows)
    base_ref[...] = total[:, :columns]

    for which in range(len(factors)):
        for i in range(1, chips):
            gather(which, i).wait_send()
        for i in range(chips):
            relayed(which, i, d).wait_send()
    for step in range(tp - 1):
        low_copy(step).wait_send()
        share_copy(step).wait_send()


def on_device(
    residual_hidden,
    attention_norm_gain,
    query_matrix,
    key_matrix,
    value_matrix,
    output_matrix,
    query_adapter_down,
    query_adapter_up,
    output_adapter_down,
    output_adapter_up,
    cached_rotated_keys,
    cached_value_rows,
    cache_fill_lengths,
):
    dp, tp = lax.axis_size("dp"), lax.axis_size("tp")
    rows, features = residual_hidden.shape
    width = query_matrix.shape[1]
    heads = width // HEAD_SIZE
    groups = key_matrix.shape[1] // HEAD_SIZE
    columns = output_matrix.shape[1] // tp
    pieces = rows
    bf16, f32 = jnp.bfloat16, jnp.float32
    operands = (
        residual_hidden,
        attention_norm_gain.reshape(1, features),
        cache_fill_lengths.reshape(1, rows),
        query_matrix,
        key_matrix,
        value_matrix,
        output_matrix,
        query_adapter_down.T,
        query_adapter_up,
        output_adapter_down.T,
        output_adapter_up,
        cached_rotated_keys,
        cached_value_rows,
    )
    base, extra = pl.pallas_call(
        functools.partial(kernel, dp, tp),
        out_shape=[pltpu.VMEM((rows, columns), f32)] * 2,
        in_specs=[pl.BlockSpec(memory_space=pl.ANY)] * len(operands),
        out_specs=[pl.BlockSpec(memory_space=pltpu.VMEM)] * 2,
        scratch_shapes=[
            pltpu.VMEM(residual_hidden.shape, bf16),
            pltpu.VMEM((1, features), f32),
            pltpu.VMEM((1, rows), jnp.int32),
            pltpu.VMEM((rows, 2 * HEAD_SIZE), f32),
            pltpu.VMEM(query_matrix.shape, bf16),
            pltpu.VMEM(key_matrix.shape, bf16),
            pltpu.VMEM(value_matrix.shape, bf16),
            pltpu.VMEM((tp, width, columns), bf16),
            pltpu.VMEM((dp,) + query_adapter_down.shape[::-1], bf16),
            pltpu.VMEM((dp,) + query_adapter_up.shape, bf16),
            pltpu.VMEM((dp,) + output_adapter_down.shape[::-1], bf16),
            pltpu.VMEM((dp,) + output_adapter_up.shape, bf16),
            pltpu.VMEM(cached_rotated_keys.shape, bf16),
            pltpu.VMEM(cached_value_rows.shape, bf16),
            pltpu.VMEM((rows, features), bf16),
            pltpu.VMEM((rows, heads, HEAD_SIZE), f32),
            pltpu.VMEM((rows, groups + 1, HEAD_SIZE), f32),
            pltpu.VMEM((rows, groups, HEAD_SIZE), f32),
            pltpu.VMEM((heads, rows, HEAD_SIZE), f32),
            pltpu.VMEM((rows, HEAD_SIZE), f32),
            pltpu.VMEM((tp - 1, rows, HEAD_SIZE), f32),
            pltpu.VMEM((tp, rows, columns + HEAD_SIZE), f32),
            pltpu.VMEM((tp - 1, rows, columns + HEAD_SIZE), f32),
            pltpu.SemaphoreType.DMA((3,)),
            pltpu.SemaphoreType.DMA((3, pieces)),
            pltpu.SemaphoreType.DMA((2, rows)),
            pltpu.SemaphoreType.DMA((tp, 2)),
            pltpu.SemaphoreType.DMA((4,)),
            pltpu.SemaphoreType.DMA((4, dp // 2)),
            pltpu.SemaphoreType.DMA((4, dp // 2)),
            pltpu.SemaphoreType.DMA((4, dp // 2)),
            pltpu.SemaphoreType.DMA((4, dp // 2)),
            pltpu.SemaphoreType.DMA((tp - 1,)),
            pltpu.SemaphoreType.DMA((tp - 1,)),
            pltpu.SemaphoreType.DMA((tp - 1,)),
            pltpu.SemaphoreType.DMA((tp - 1,)),
        ],
        compiler_params=pltpu.CompilerParams(
            collective_id=0, has_side_effects=True, vmem_limit_bytes=56 * 1024 * 1024
        ),
    )(*operands)
    return base + extra


def solution(mesh):
    in_specs = (
        P("dp", None),
        P(),
        P(None, "tp"),
        P(None, "tp"),
        P(None, "tp"),
        P("tp", None),
        P(("dp", "tp"), None),
        P(None, ("tp", "dp")),
        P(("tp", "dp"), None),
        P(None, ("tp", "dp")),
        P("dp", "tp", None, None),
        P("dp", "tp", None, None),
        P("dp"),
    )
    out_specs = P("dp", "tp")

    def local(*arrays):
        wide = arrays[7].shape[1] % HEAD_SIZE == 0 and arrays[9].shape[1] % HEAD_SIZE == 0
        return (on_device if wide else on_device_narrow)(*arrays)

    return jax.shard_map(
        local, mesh=mesh, in_specs=in_specs, out_specs=out_specs, check_vma=False
    )
```
